512 devices in a mesh: layer: 2 (over x_hi), feat: 64 (over y, z), tok: 4 (over x_lo, core).
Axes of the slice: x: 4 (x_hi: 2, x_lo: 2; x = x_hi * 2 + x_lo), y: 8, z: 8, core: 2. Of those that a mesh axis runs over, the one named last changes fastest.
Arguments:
- resid: bfloat16 [2, 1024, 2304], P('layer', 'tok', 'feat'), may hold values from -6 to 6
- norm_gain: bfloat16 [2, 2304], P('layer', 'feat'), may hold values from 0.5 to 2
- prev_codes: bfloat16 [1024, 16384], P('tok', 'feat'), may hold values from 0 to 1.5
- feature_mask: int32 [2, 8, 128], P('layer', 'tok', 'feat'), may hold values 0 or 1
- w_gate: bfloat16 [2, 2304, 9216], P('layer', 'tok', 'feat'), may hold values from -0.125 to 0.125
- w_up: bfloat16 [2, 2304, 9216], P('layer', 'tok', 'feat'), may hold values from -0.125 to 0.125
- w_down: bfloat16 [2, 9216, 2304], P('layer', 'feat', 'tok'), may hold values from -0.0625 to 0.0625
- enc_weight: bfloat16 [2, 2304, 16384], P('layer', 'tok', 'feat'), may hold values from -0.125 to 0.125
- enc_bias: float32 [2, 16384], P('layer', 'feat'), may hold values from -3 to 3
- dec_own: bfloat16 [2, 16384, 2304], P('layer', 'feat', 'tok'), may hold values from -0.046875 to 0.046875
- dec_prev: bfloat16 [2, 16384, 2304], P('layer', 'feat', 'tok'), may hold values from -0.046875 to 0.046875
Outputs:
- grad_enc: float32 [2, 2304, 16384], P('layer', 'tok', 'feat')
- grad_bias: float32 [2, 16384], P('layer', 'feat')
- grad_own: float32 [2, 16384, 2304], P('layer', 'feat', 'tok')
- grad_prev: float32 [2, 16384, 2304], P('layer', 'feat', 'tok')
The draws below stay inside these ranges and needn't reach their ends.
All inputs are finite; a program needn't handle non-finite values. No bound on the sum of `feature_mask` on one device may be relied on, other than what follows from the above.
Results may differ from the reference program's by a relative error of at most 0.0063.
Values may be sent and summed in bfloat16 or wider, within the bound.
No kernel may reach another device: no remote copies, remote signals or barrier semaphores. Data moves between devices by JAX's collectives and lax.ppermute only.
A program may use at most 64 MiB of HBM per device.

```python
import math
import jax
import jax.numpy as jnp
from jax import lax

D = 2304
FF = 9216
F = 16384
TILE = 128
TBLK = 128
TOKENS = 1024
LAYERS = 2


def with_ends(values, rng, least, high):
    longest = values.shape.index(max(values.shape))
    spots = []
    for shift in (0, 1):
        where = [jax.random.randint(jax.random.fold_in(rng, axis), (), 0, length) for axis, length in enumerate(values.shape)]
        where[longest] = (where[longest] + shift) % values.shape[longest]
        spots.append(tuple(where))
    return values.at[spots[0]].set(least).at[spots[1]].set(high)


def steps_of(own_key, shape, pieces, smallest, top_value):
    gain = 1.0
    for axis_at, parts in pieces:
        heights = jax.random.uniform(jax.random.fold_in(jax.random.fold_in(own_key, 6), axis_at), (parts,), jnp.float32, smallest / len(pieces), top_value / len(pieces))
        gain = gain * jnp.repeat(jnp.exp(heights), shape[axis_at] // parts).reshape((-1,) + (1,) * (len(shape) - 1 - axis_at))
    return gain


def gaussian(key, shape, deviation, limit, shards=(), held_as=jnp.bfloat16):
    entries = deviation * jax.random.normal(key, shape, jnp.float32)
    if shards:
        entries = entries * steps_of(key, shape, shards, -0.22, 0.18)
    return jnp.clip(entries, -limit, limit).astype(held_as)


def setup_inputs(seed: int = 0) -> dict:
    key_of = jax.random.split(jax.random.key(seed), 12)
    return {
        "resid": gaussian(key_of[0], (LAYERS, TOKENS, D), 1.0, 6.0, ((0, 2), (1, 4), (2, 64))),
        "norm_gain": jnp.clip(0.5 + 1.5 * jax.random.uniform(key_of[1], (LAYERS, D), jnp.float32) ** steps_of(key_of[1], (LAYERS, D), ((0, 2), (1, 64)), -0.2, 0.2), 0.5, 2.0).astype(jnp.bfloat16),
        "prev_codes": jnp.clip(1.5 * jax.random.uniform(key_of[2], (TOKENS, F), jnp.float32) ** steps_of(key_of[2], (TOKENS, F), ((0, 4), (1, 64)), -0.2, 0.2), 0.0, 1.5).astype(jnp.bfloat16),
        "feature_mask": with_ends((jax.random.randint(key_of[3], (LAYERS, TOKENS // TBLK, F // TILE), 0, 4) < 3).astype(jnp.int32), jax.random.fold_in(key_of[3], 1), 0, 1),
        "w_gate": gaussian(key_of[4], (LAYERS, D, FF), D ** -0.5, 0.125, ((0, 2), (1, 4), (2, 64))),
        "w_up": gaussian(key_of[5], (LAYERS, D, FF), D ** -0.5, 0.125, ((0, 2), (1, 4), (2, 64))),
        "w_down": gaussian(key_of[6], (LAYERS, FF, D), FF ** -0.5, 0.0625, ((0, 2), (1, 64), (2, 4))),
        "enc_weight": gaussian(key_of[7], (LAYERS, D, F), D ** -0.5, 0.125, ((0, 2), (1, 4), (2, 64))),
        "enc_bias": gaussian(key_of[8], (LAYERS, F), 0.5, 3.0, ((0, 2), (1, 64)), jnp.float32),
        "dec_own": gaussian(key_of[9], (LAYERS, F, D), F ** -0.5, 0.046875, ((0, 2), (1, 64), (2, 4))),
        "dec_prev": gaussian(key_of[10], (LAYERS, F, D), F ** -0.5, 0.046875, ((0, 2), (1, 64), (2, 4))),
    }


def expand_mask(block_mask):
    grown = jnp.repeat(jnp.repeat(block_mask, TBLK, axis=0), TILE, axis=1)
    return grown.astype(jnp.float32)

def reference(resid, norm_gain, prev_codes, feature_mask, w_gate, w_up, w_down, enc_weight, enc_bias, dec_own, dec_prev):
    factor = 1.0 / math.sqrt(TOKENS)
    normed_list = []
    codes_list = []
    source_list = []
    active_list = []
    keeper_list = []
    error_list = []
    for layer_idx in range(LAYERS):
        stream = resid[layer_idx].astype(jnp.float32)
        normed = (stream * lax.rsqrt(lax.optimization_barrier(jnp.mean(stream * stream, axis=1, keepdims=True)) + 1e-06) * norm_gain[layer_idx].astype(jnp.float32)).astype(jnp.bfloat16)
        gate_sum = jnp.dot(normed, w_gate[layer_idx], preferred_element_type=jnp.float32)
        up_sum = jnp.dot(normed, w_up[layer_idx], preferred_element_type=jnp.float32)
        hidden = (jax.nn.gelu(gate_sum, approximate=True) * up_sum).astype(jnp.bfloat16)
        preact = jnp.dot(normed, enc_weight[layer_idx], preferred_element_type=jnp.float32) + enc_bias[layer_idx]
        active = jnp.maximum(preact, 0.0)
        keeper = expand_mask(feature_mask[layer_idx])
        codes = (active * active * keeper).astype(jnp.bfloat16)
        source = prev_codes if layer_idx == 0 else codes_list[-1]
        partial_value = jnp.dot(codes, dec_own[layer_idx], preferred_element_type=jnp.float32) + jnp.dot(source, dec_prev[layer_idx], preferred_element_type=jnp.float32) - jnp.dot(hidden, w_down[layer_idx], preferred_element_type=jnp.float32)
        normed_list.append(normed)
        codes_list.append(codes)
        source_list.append(source)
        active_list.append(active)
        keeper_list.append(keeper)
        error_list.append(partial_value.astype(jnp.bfloat16))
    grads_enc = []
    grads_bias = []
    grads_own = []
    grads_prev = []
    for layer_idx in range(LAYERS):
        error = error_list[layer_idx]
        back = jnp.dot(error, dec_own[layer_idx].T, preferred_element_type=jnp.float32)
        if layer_idx + 1 < LAYERS:
            back = back + jnp.dot(error_list[layer_idx + 1], dec_prev[layer_idx + 1].T, preferred_element_type=jnp.float32)
        pregrad = (back * keeper_list[layer_idx] * (2.0 * active_list[layer_idx]) * factor).astype(jnp.bfloat16)
        grads_enc.append(jnp.dot(normed_list[layer_idx].T, pregrad, preferred_element_type=jnp.float32))
        grads_bias.append(lax.optimization_barrier(jnp.sum(pregrad.astype(jnp.float32), axis=0)))
        grads_own.append(jnp.dot(codes_list[layer_idx].T, error, preferred_element_type=jnp.float32) * factor)
        grads_prev.append(jnp.dot(source_list[layer_idx].T, error, preferred_element_type=jnp.float32) * factor)
    return (jnp.stack(grads_enc), jnp.stack(grads_bias), jnp.stack(grads_own), jnp.stack(grads_prev))
```

```python
import math

import jax
import jax.numpy as jnp
from jax import lax
from jax.experimental import pallas as pl
from jax.experimental.pallas import tpu as pltpu
from jax.sharding import Mesh
from jax.sharding import PartitionSpec as P

TILE = 128
TBLK = 128
BF = jnp.bfloat16
F32 = jnp.float32
TOK = ("tok_0", "tok_1")
PARAMS = pltpu.CompilerParams(vmem_limit_bytes=56 * 1024 * 1024)
VM = pl.BlockSpec(memory_space=pltpu.VMEM)
SM = pl.BlockSpec(memory_space=pltpu.SMEM)


def call(kernel, ins, outs, scratch=()):
    specs = [SM if a.dtype == jnp.int32 else VM for a in ins]
    return pl.pallas_call(
        kernel,
        out_shape=[jax.ShapeDtypeStruct(s, d) for s, d in outs],
        in_specs=specs,
        out_specs=[VM] * len(outs),
        scratch_shapes=list(scratch),
        compiler_params=PARAMS,
    )(*ins)


def dot(a, b, ca=1, cb=0):
    return lax.dot_general(a, b, (((ca,), (cb,)), ((), ())), preferred_element_type=F32)


def swap(x, axis):
    return lax.ppermute(x, axis, [(0, 1), (1, 0)])


def gather4(x):
    far = swap(x, "tok_0")
    near = swap(x, "tok_1")
    return [x, near, far, swap(far, "tok_1")]


def exchange(blocks, axis):
    return lax.all_to_all(blocks, axis, split_axis=0, concat_axis=0, tiled=True)


def spread_kernel(x_ref, o_ref):
    turned = x_ref[...].astype(F32).T
    half = turned.shape[1] // 2
    both = jnp.concatenate([turned[:, :half], turned[:, half:]], axis=0).astype(BF)
    o_ref[...] = jnp.broadcast_to(both[None], o_ref.shape)


def encode_kernel(
    t_ref, mask_ref, g_ref, gain_ref, w0, w1, w2, w3, bias_ref,
    nt_ref, codes_ref, slope_ref, hidden_ref, x_ref,
):
    feats, rows2, lanes = g_ref.shape
    rows = rows2 // 2
    for f in range(feats):
        for h in range(2):
            x_ref[pl.ds(f * rows, rows), pl.ds(h * lanes, lanes)] = g_ref[
                f, pl.ds(h * rows, rows), :
            ].astype(F32)
    depth = feats * rows
    block = depth // 4
    total = jnp.zeros((1, 2 * lanes), F32)
    for k in range(4):
        x = x_ref[pl.ds(k * block, block), :]
        total = total + jnp.sum(x * x, axis=0, keepdims=True)
    scale = lax.rsqrt(total / depth + 1e-06)
    for k in range(4):
        at = pl.ds(k * block, block)
        gain = gain_ref[at, :].astype(F32)
        for h in range(2):
            lane = pl.ds(h * lanes, lanes)
            value = x_ref[at, lane] * scale[:, h * lanes : (h + 1) * lanes] * gain
            nt_ref[k, :, lane] = value.astype(BF)
    t = t_ref[0]
    width = bias_ref.shape[1]
    sums = dot(nt_ref[t], w0[...], 0, 0)
    for k, w in ((1, w1), (2, w2), (3, w3)):
        sums += dot(nt_ref[jnp.bitwise_xor(t, k)], w[...], 0, 0)
    units = hidden_ref.shape[1]
    preact = sums[:, :width] + bias_ref[...]
    active = jnp.maximum(preact, 0.0)
    factor = 1.0 / math.sqrt(4 * codes_ref.shape[0])
    for i in range(codes_ref.shape[0] // TBLK):
        for j in range(width // TILE):
            keep = mask_ref[i, j].astype(F32)
            r, c = slice(i * TBLK, (i + 1) * TBLK), slice(j * TILE, (j + 1) * TILE)
            part = active[r, c]
            codes_ref[r, c] = (part * part * keep).astype(BF)
            slope_ref[r, c] = part * (keep * (2.0 * factor))
    gate, up = sums[:, width : width + units], sums[:, width + units :]
    hidden_ref[...] = (jax.nn.gelu(gate, approximate=True) * up).astype(BF)


def decode_kernel(t_ref, codes_ref, source_ref, hidden_ref, w0, w1, w2, w3, o_ref, s_ref):
    t = t_ref[0]
    n = codes_ref.shape[1]
    codes, source, hidden = codes_ref[...], source_ref[...], hidden_ref[...]
    for k, w in enumerate((w0, w1, w2, w3)):
        value = dot(codes, w[:n]) + dot(source, w[n : 2 * n]) - dot(hidden, w[2 * n :])
        s_ref[jnp.bitwise_xor(t, k)] = value
    peers, rows, cols = o_ref.shape
    for h in range(2):
        both = jnp.concatenate([s_ref[2 * h], s_ref[2 * h + 1]], axis=1)
        o_ref[pl.ds(h * peers // 2, peers // 2)] = both.reshape(peers // 2, rows, cols).astype(BF)


def total_kernel(x_ref, o_ref):
    total = jnp.sum(x_ref[...].astype(F32), axis=0).astype(BF)
    o_ref[...] = jnp.broadcast_to(total[None], o_ref.shape)


def back_kernel(t_ref, e_ref, w0, w1, w2, w3, own_ref, prev_ref, err_ref):
    t = t_ref[0]
    peers, rows, cols = e_ref.shape
    n = own_ref.shape[1]
    for h in range(2):
        e = e_ref[pl.ds(h * peers // 2, peers // 2)].astype(F32).reshape(peers // 2 * rows, cols)
        err_ref[2 * h] = e[:, : cols // 2].astype(BF)
        err_ref[2 * h + 1] = e[:, cols // 2 :].astype(BF)
    total = dot(err_ref[t], w0[: 2 * n], 1, 1)
    for k, w in ((1, w1), (2, w2), (3, w3)):
        total += dot(err_ref[jnp.bitwise_xor(t, k)], w[: 2 * n], 1, 1)
    own_ref[...] = total[:, :n]
    prev_ref[...] = total[:, n:].astype(BF)


def decoder_grads_kernel(t_ref, e_ref, c0, c1, c2, c3, own_ref, prev_ref):
    t = t_ref[0]
    n = own_ref.shape[0]
    factor = 1.0 / math.sqrt(4 * e_ref.shape[1])
    total = dot(c0[...], e_ref[t], 0, 0)
    for k, c in ((1, c1), (2, c2), (3, c3)):
        total += dot(c[...], e_ref[jnp.bitwise_xor(t, k)], 0, 0)
    own_ref[...] = total[:n] * factor
    prev_ref[...] = total[n:] * factor


def encoder_grads_kernel(t_ref, n_ref, p0, p1, p2, p3, grad_ref, bias_ref):
    t = t_ref[0]
    total = dot(n_ref[t], p0[...])
    bias = jnp.sum(p0[...].astype(F32), axis=0, keepdims=True)
    for k, p in ((1, p1), (2, p2), (3, p3)):
        total += dot(n_ref[jnp.bitwise_xor(t, k)], p[...])
        bias += jnp.sum(p[...].astype(F32), axis=0, keepdims=True)
    grad_ref[...] = total
    bias_ref[...] = bias


def local(
    resid,
    norm_gain,
    prev_codes,
    feature_mask,
    w_gate,
    w_up,
    w_down,
    enc_weight,
    enc_bias,
    dec_own,
    dec_prev,
):
    height, strip = resid.shape[1:]
    peers = lax.axis_size("feat")
    depth = strip * peers
    width = enc_weight.shape[2]
    units = w_gate.shape[2]
    block = depth // 4
    t = (2 * lax.axis_index("tok_0") + lax.axis_index("tok_1")).astype(jnp.int32).reshape(1)

    (copies,) = call(spread_kernel, (resid[0],), [((peers, 2 * strip, height // 2), BF)])
    gathered = exchange(copies, "feat")
    gains = exchange(jnp.broadcast_to(norm_gain[:, None], (peers, 1, strip)), "feat")
    gain_rows = jnp.broadcast_to(gains.reshape(depth, 1), (depth, 128))

    first = gather4(jnp.concatenate([enc_weight[0], w_gate[0], w_up[0]], axis=1))
    second = gather4(jnp.concatenate([dec_own[0], dec_prev[0], w_down[0]], axis=0))

    turned, codes, slope, hidden = call(
        encode_kernel,
        (t, feature_mask[0], gathered, gain_rows, *first, enc_bias),
        [
            ((4, block, height), BF),
            ((height, width), BF),
            ((height, width), F32),
            ((height, units), BF),
        ],
        [pltpu.VMEM((depth, height), F32)],
    )
    shifted = lax.ppermute(codes, "layer", [(0, 1)])
    source = jnp.where(lax.axis_index("layer") == 0, prev_codes, shifted)
    (parts,) = call(
        decode_kernel,
        (t, codes, source, hidden, *second),
        [((peers, height * 2 // peers, depth // 2), BF)],
        [pltpu.VMEM((4, height, block), F32)],
    )
    arrived = exchange(parts, "feat")
    turned_cols = exchange(turned, TOK)
    both_codes = gather4(jnp.concatenate([codes, source], axis=1))
    (copies,) = call(total_kernel, (arrived,), [(parts.shape, BF)])
    errors = exchange(copies, "feat")
    own_back, prev_back, err = call(
        back_kernel,
        (t, errors, *second),
        [((height, width), F32), ((height, width), BF), ((4, height, block), BF)],
    )
    later = lax.ppermute(prev_back, "layer", [(1, 0)]).astype(F32)
    err_cols = exchange(err, TOK)
    pregrad = gather4(((own_back + later) * slope).astype(BF))
    grad_own, grad_prev = call(
        decoder_grads_kernel,
        (t, err_cols, *both_codes),
        [((width, block), F32), ((width, block), F32)],
    )
    grad_enc, grad_bias = call(
        encoder_grads_kernel,
        (t, turned_cols, *pregrad),
        [((block, width), F32), ((1, width), F32)],
    )
    return (grad_enc[None], grad_bias, grad_own[None], grad_prev[None])


def solution(mesh):
    split = Mesh(
        mesh.devices.reshape(mesh.shape["layer"], mesh.shape["feat"], 2, 2),
        ("layer", "feat", "tok_0", "tok_1"),
    )
    placed = (
        P("layer", TOK, "feat"),
        P("layer", "feat"),
        P(TOK, "feat"),
        P("layer", TOK, "feat"),
        P("layer", TOK, "feat"),
        P("layer", TOK, "feat"),
        P("layer", "feat", TOK),
        P("layer", TOK, "feat"),
        P("layer", "feat"),
        P("layer", "feat", TOK),
        P("layer", "feat", TOK),
    )
    return jax.shard_map(
        local,
        mesh=split,
        in_specs=placed,
        out_specs=(
            P("layer", TOK, "feat"),
            P("layer", "feat"),
            P("layer", "feat", TOK),
            P("layer", "feat", TOK),
        ),
        check_vma=False,
    )
```

```python
import math

import jax
import jax.numpy as jnp
from jax import lax
from jax.experimental import pallas as pl
from jax.experimental.pallas import tpu as pltpu
from jax.sharding import Mesh
from jax.sharding import PartitionSpec as P

TILE = 128
TBLK = 128
BF = jnp.bfloat16
F32 = jnp.float32
TOK = ("tok_0", "tok_1")
PARAMS = pltpu.CompilerParams(vmem_limit_bytes=56 * 1024 * 1024)
VM = pl.BlockSpec(memory_space=pltpu.VMEM)
SM = pl.BlockSpec(memory_space=pltpu.SMEM)


ANY = pl.BlockSpec(memory_space=pl.ANY)
PITCH = 40
ROWS = 72


def call(kernel, ins, outs, scratch=(), after=()):
    specs = [SM if a.dtype == jnp.int32 else VM for a in ins] + [ANY] * len(after)
    count = len(ins)

    def body(*refs):
        kernel(*refs[:count], *refs[count + len(after) :])

    return pl.pallas_call(
        body,
        out_shape=[jax.ShapeDtypeStruct(s, d) for s, d in outs],
        in_specs=specs,
        out_specs=[VM] * len(outs),
        scratch_shapes=list(scratch),
        compiler_params=PARAMS,
        name=kernel.__name__,
    )(*ins, *after)


def dot(a, b, ca=1, cb=0):
    return lax.dot_general(a, b, (((ca,), (cb,)), ((), ())), preferred_element_type=F32)


def toward(x, k):
    return lax.ppermute(x, TOK, [(i, i ^ k) for i in range(4)])


def gather4(x):
    far = toward(x, 2)
    return [x, toward(x, 1), far, toward(far, 1)]


def exchange4(blocks):
    return [blocks[0]] + [toward(blocks[k], k) for k in (1, 2, 3)]


def exchange(blocks):
    return lax.all_to_all(blocks, "feat", split_axis=0, concat_axis=0, tiled=True)


def spread_kernel(x_ref, gain_ref, o_ref):
    strip, height = x_ref.shape
    lanes = height // 2
    x = x_ref[...].astype(F32)
    gain = gain_ref[...].astype(F32)
    row = jnp.concatenate([gain, jnp.zeros((1, lanes - strip), F32)], axis=1)
    rest = jnp.zeros((PITCH - strip - 1, lanes), F32)
    parts = [x[:, :lanes], row, rest, x[:, lanes:], row, rest]
    o_ref[...] = jnp.broadcast_to(jnp.concatenate(parts, axis=0).astype(BF)[None], o_ref.shape)


def put_wide(o_ref, at, w):
    rows, cols = w.shape
    for c in range(0, cols, 128):
        wide = min(128, cols - c)
        o_ref[pl.ds(at, rows), pl.ds(0, wide)] = w[:, c : c + wide]
        at += rows
    return at


def get_wide(w_ref, at, rows, cols):
    pieces = [
        w_ref[pl.ds(at + rows * i, rows), : min(128, cols - 128 * i)] for i in range(-(-cols // 128))
    ]
    return jnp.concatenate(pieces, axis=1)


def pack_kernel(enc, gate, up, own, prev, down, before, first_ref, second_ref, before_ref):
    at = 0
    for w in (enc, gate, up):
        at = put_wide(first_ref, at, w[...])
    at = 0
    for w in (own, prev, down):
        at = put_wide(second_ref, at, w[...])
    before_ref[...] = before[...].astype(F32).T.astype(BF)


def encode_kernel(
    t_ref, mask_ref, g_ref, w0, w1, w2, w3, bias_ref,
    n0, n1, n2, n3, codes_ref, slope_ref, hidden_ref, x_ref,
):
    feats, _, lanes = g_ref.shape
    height = 2 * lanes
    block = n0.shape[0]
    strip = 4 * block // feats
    depth = feats * strip
    width = codes_ref.shape[0]
    units = hidden_ref.shape[0]
    gains = g_ref[:, strip, :].astype(F32).T
    total = jnp.zeros((8, height), F32)
    for f in range(feats):
        x = jnp.concatenate(
            [g_ref[f, pl.ds(0, strip), :], g_ref[f, pl.ds(PITCH, strip), :]], axis=1
        ).astype(F32)
        square = x * x
        for r in range(0, strip - 7, 8):
            total = total + square[r : r + 8]
        tail = square[strip // 8 * 8 :]
        total = total + jnp.concatenate([tail, jnp.zeros_like(tail)], axis=0)
        x_ref[pl.ds(f * strip, strip), :] = x * gains[:strip, f : f + 1]
    total = jnp.sum(total, axis=0, keepdims=True)
    scale = lax.rsqrt(total / depth + 1e-06)
    t = t_ref[0]
    sums = gate = up = 0.0
    for k, (n_ref, w) in enumerate(((n0, w0), (n1, w1), (n2, w2), (n3, w3))):
        at = pl.ds(pl.multiple_of(jnp.bitwise_xor(t, k) * block, 64), block)
        n = (x_ref[at, :] * scale).astype(BF)
        n_ref[...] = n
        sums += dot(get_wide(w, 0, block, width), n, 0, 0)
        base = block * width // 128
        gate += dot(get_wide(w, base, units, block), n)
        up += dot(get_wide(w, base + units * (-(-block // 128)), units, block), n)
    bias = jnp.broadcast_to(bias_ref[...], (128, width)).T
    factor = 1.0 / math.sqrt(4 * height)
    for j in range(width // TILE):
        for i in range(height // TBLK):
            keep = mask_ref[i, j].astype(F32)
            r, c = slice(j * TILE, (j + 1) * TILE), slice(i * TBLK, (i + 1) * TBLK)
            part = jnp.maximum(sums[r, c] + bias[r, :], 0.0)
            codes_ref[r, c] = (part * part * keep).astype(BF)
            slope_ref[r, c] = part * (keep * (2.0 * factor))
    hidden_ref[...] = (jax.nn.gelu(gate, approximate=True) * up).astype(BF)


def decode_kernel(
    t_ref, codes_ref, before_ref, shifted_ref, hidden_ref, w0, w1, w2, w3, o_ref, both_ref
):
    t, layer = t_ref[0], t_ref[1]
    n = codes_ref.shape[0]
    units = hidden_ref.shape[0]
    block = o_ref.shape[0] * ROWS // 8
    both_ref[:n] = codes_ref[...]

    @pl.when(layer == 0)
    def _():
        both_ref[n:] = before_ref[...]

    @pl.when(layer != 0)
    def _():
        both_ref[n:] = shifted_ref[...]

    both, hidden = both_ref[...], hidden_ref[...]
    peers, rows, lanes = o_ref.shape
    each = block // rows
    for k, w in enumerate((w0, w1, w2, w3)):
        decoder = jnp.concatenate(
            [get_wide(w, 0, block, n), get_wide(w, block * n // 128, block, n)], axis=1
        )
        down = get_wide(w, 2 * block * n // 128, units, block)
        value = dot(decoder, both) - dot(down, hidden, 0, 0)
        spot = jnp.bitwise_xor(t, k) * each
        for i in range(each):
            for h in range(2):
                o_ref[spot + (h * peers // 2 + i)] = value[
                    i * rows : (i + 1) * rows, h * lanes : (h + 1) * lanes
                ].astype(BF)


def total_kernel(x_ref, o_ref):
    total = jnp.sum(x_ref[...].astype(F32), axis=0).astype(BF)
    o_ref[...] = jnp.broadcast_to(total[None], o_ref.shape)


def back_kernel(t_ref, e_ref, w0, w1, w2, w3, own_ref, prev_ref, e0, e1, e2, e3):
    t = t_ref[0]
    peers, rows, lanes = e_ref.shape
    n = own_ref.shape[0]
    block = e0.shape[0]
    each = block // rows
    total = 0.0
    for k, (err_ref, w) in enumerate(((e0, w0), (e1, w1), (e2, w2), (e3, w3))):
        spot = jnp.bitwise_xor(t, k) * each
        half = [
            jnp.concatenate(
                [e_ref[spot + (h * peers // 2 + i)].astype(F32) for i in range(each)], axis=0
            ).astype(BF)
            for h in range(2)
        ]
        err = jnp.concatenate(half, axis=1)
        err_ref[...] = err
        decoder = jnp.concatenate(
            [get_wide(w, 0, block, n), get_wide(w, block * n // 128, block, n)], axis=1
        )
        total += dot(decoder, err, 0, 0)
    own_ref[...] = total[:n]
    prev_ref[...] = total[n:].astype(BF)


def decoder_grads_kernel(e0, e1, e2, e3, c0, c1, c2, c3, own_ref, prev_ref):
    n = own_ref.shape[1]
    factor = 1.0 / math.sqrt(4 * e0.shape[1])
    total = 0.0
    for e, c in ((e0, c0), (e1, c1), (e2, c2), (e3, c3)):
        total += dot(e[...], c[...], 1, 1)
    own_ref[...] = total[:, :n] * factor
    prev_ref[...] = total[:, n:] * factor


def encoder_grads_kernel(n0, n1, n2, n3, p0, p1, p2, p3, grad_ref, bias_ref):
    total = bias = 0.0
    ones = jnp.ones((8, p0.shape[1]), BF)
    for n, p in ((n0, p0), (n1, p1), (n2, p2), (n3, p3)):
        total += dot(n[...], p[...], 1, 1)
        bias += dot(ones, p[...], 1, 1)
    grad_ref[...] = total
    bias_ref[...] = bias[:1]


def local(
    resid,
    norm_gain,
    prev_codes,
    feature_mask,
    w_gate,
    w_up,
    w_down,
    enc_weight,
    enc_bias,
    dec_own,
    dec_prev,
):
    height, strip = resid.shape[1:]
    peers = lax.axis_size("feat")
    width = enc_weight.shape[2]
    units = w_gate.shape[2]
    block = strip * peers // 4
    spans = -(-block // 128)
    t = 2 * lax.axis_index("tok_0") + lax.axis_index("tok_1")
    place = jnp.stack([t, lax.axis_index("layer")]).astype(jnp.int32)
    flip = lambda a: jnp.swapaxes(a[0], 0, 1)

    (copies,) = call(
        spread_kernel, (flip(resid), norm_gain), [((peers, 2 * PITCH, height // 2), BF)]
    )
    gathered = exchange(copies)
    first, second, before = call(
        pack_kernel,
        (
            enc_weight[0], flip(w_gate), flip(w_up),
            flip(dec_own), flip(dec_prev), w_down[0], prev_codes,
        ),
        [
            ((block * width // 128 + 2 * units * spans, 128), BF),
            ((2 * block * width // 128 + units * spans, 128), BF),
            ((width, height), BF),
        ],
    )
    first = gather4(first)
    second = gather4(second)
    *normed, codes, slope, hidden = call(
        encode_kernel,
        (place, feature_mask[0], gathered, *first, enc_bias),
        [((block, height), BF)] * 4
        + [((width, height), BF), ((width, height), F32), ((units, height), BF)],
        [pltpu.VMEM((4 * block, height), F32)],
    )
    shifted = lax.ppermute(codes, "layer", [(0, 1)])
    parts, both = call(
        decode_kernel,
        (place, codes, before, shifted, hidden, *second),
        [((peers, ROWS, height // 2), BF), ((2 * width, height), BF)],
    )
    arrived = exchange(parts)
    normed = exchange4(normed)
    (copies,) = call(total_kernel, (arrived,), [(parts.shape, BF)], after=normed[1:])
    errors = exchange(copies)
    both = gather4(both)
    own_back, prev_back, *err = call(
        back_kernel,
        (place, errors, *second),
        [((width, height), F32), ((width, height), BF)] + [((block, height), BF)] * 4,
        after=both[1:],
    )
    later = lax.ppermute(prev_back, "layer", [(1, 0)]).astype(F32)
    err = exchange4(err)
    pregrad = gather4(((own_back + later) * slope).astype(BF))
    grad_own, grad_prev = call(
        decoder_grads_kernel, (*err, *both), [((block, width), F32)] * 2
    )
    grad_enc, grad_bias = call(
        encoder_grads_kernel,
        (*normed, *pregrad),
        [((block, width), F32), ((1, width), F32)],
    )
    return (grad_enc[None], grad_bias, grad_own.T[None], grad_prev.T[None])


def solution(mesh):
    split = Mesh(
        mesh.devices.reshape(mesh.shape["layer"], mesh.shape["feat"], 2, 2),
        ("layer", "feat", "tok_0", "tok_1"),
    )
    placed = (
        P("layer", TOK, "feat"),
        P("layer", "feat"),
        P(TOK, "feat"),
        P("layer", TOK, "feat"),
        P("layer", TOK, "feat"),
        P("layer", TOK, "feat"),
        P("layer", "feat", TOK),
        P("layer", TOK, "feat"),
        P("layer", "feat"),
        P("layer", "feat", TOK),
        P("layer", "feat", TOK),
    )
    return jax.shard_map(
        local,
        mesh=split,
        in_specs=placed,
        out_specs=(
            P("layer", TOK, "feat"),
            P("layer", "feat"),
            P("layer", "feat", TOK),
            P("layer", "feat", TOK),
        ),
        check_vma=False,
    )
```

```python
import math

import jax
import jax.numpy as jnp
from jax import lax
from jax.experimental import pallas as pl
from jax.experimental.pallas import tpu as pltpu
from jax.sharding import Mesh
from jax.sharding import PartitionSpec as P

TILE = 128
TBLK = 128
BF = jnp.bfloat16
F32 = jnp.float32
TOK = ("tok_0", "tok_1")
PARAMS = pltpu.CompilerParams(vmem_limit_bytes=56 * 1024 * 1024)
VM = pl.BlockSpec(memory_space=pltpu.VMEM)
SM = pl.BlockSpec(memory_space=pltpu.SMEM)


ANY = pl.BlockSpec(memory_space=pl.ANY)
PITCH = 40
ROWS = 72


class Late:
    def __init__(self, array, low=0, high=None):
        self.array, self.low = array, low
        self.rows = (array.shape[0] if high is None else high) - low


class Coming:
    def __init__(self, source, held, sem, late):
        if late.rows != source.shape[0]:
            source = source.at[pl.ds(late.low, late.rows)]
        self.copy, self.held = pltpu.make_async_copy(source, held, sem), held

    def get(self):
        self.copy.wait()
        return self.held


def call(kernel, ins, outs, scratch=(), late=(), after=(), through=()):
    specs = [SM if a.dtype == jnp.int32 else VM for a in ins]
    specs += [ANY] * (len(late) + len(after) + len(through))
    n, m, p = len(ins), len(late), len(through)
    skip = n + m + len(after)

    def body(*refs):
        given, sources, rest = refs[:n], refs[n : n + m], refs[skip + p :]
        rest = (*rest[: len(outs)], *rest[len(outs) + p :])
        if m:
            held, sems, rest = rest[-m - 1 : -1], rest[-1], rest[: -m - 1]
        coming = [
            Coming(source, held[i], sems.at[i], late[i]) for i, source in enumerate(sources)
        ]
        for c in coming:
            c.copy.start()
        kernel(*given, *coming, *rest)

    held = [pltpu.VMEM((a.rows, *a.array.shape[1:]), a.array.dtype) for a in late]
    sems = [pltpu.SemaphoreType.DMA((m,))] if m else []
    return pl.pallas_call(
        body,
        out_shape=[jax.ShapeDtypeStruct(s, d) for s, d in outs]
        + [jax.ShapeDtypeStruct(a.shape, a.dtype) for a in through],
        in_specs=specs,
        out_specs=[VM] * len(outs) + [ANY] * p,
        input_output_aliases={skip + i: len(outs) + i for i in range(p)},
        scratch_shapes=[*scratch, *held, *sems],
        compiler_params=PARAMS,
        name=kernel.__name__,
    )(*ins, *(a.array for a in late), *after, *through)


def dot(a, b, ca=1, cb=0):
    return lax.dot_general(a, b, (((ca,), (cb,)), ((), ())), preferred_element_type=F32)


def toward(x, k):
    return lax.ppermute(x, TOK, [(i, i ^ k) for i in range(4)])


def gather4(x):
    far = toward(x, 2)
    return [x, toward(x, 1), far, toward(far, 1)]


def exchange4(blocks):
    return [blocks[0]] + [toward(blocks[k], k) for k in (1, 2, 3)]


def exchange(blocks, axis="feat"):
    return lax.all_to_all(blocks, axis, split_axis=0, concat_axis=0, tiled=True)


def spread_kernel(x_ref, gain_ref, o_ref):
    strip, height = x_ref.shape
    lanes = height // 2
    x = x_ref[...].astype(F32)
    gain = gain_ref[...].astype(F32)
    row = jnp.concatenate([gain, jnp.zeros((1, lanes - strip), F32)], axis=1)
    rest = jnp.zeros((PITCH - strip - 1, lanes), F32)
    parts = [x[:, :lanes], row, rest, x[:, lanes:], row, rest]
    o_ref[...] = jnp.broadcast_to(jnp.concatenate(parts, axis=0).astype(BF)[None], o_ref.shape)


def put_wide(o_ref, at, w):
    rows, cols = w.shape
    for c in range(0, cols, 128):
        wide = min(128, cols - c)
        o_ref[pl.ds(at, rows), pl.ds(0, wide)] = w[:, c : c + wide]
        at += rows
    return at


def get_wide(w_ref, at, rows, cols):
    pieces = [
        w_ref[pl.ds(at + rows * i, rows), : min(128, cols - 128 * i)] for i in range(-(-cols // 128))
    ]
    return jnp.concatenate(pieces, axis=1)


def pack_kernel(*refs):
    *ws, o_ref = refs
    at = 0
    for w in ws:
        at = put_wide(o_ref, at, w[...])


def pack_turn_kernel(*refs):
    *ws, x_ref, o_ref, turned_ref = refs
    pack_kernel(*ws, o_ref)
    turned_ref[...] = x_ref[...].astype(F32).T.astype(BF)


def turn_first_kernel(w0, w1, w2, w3, enc_ref, down_ref):
    _, width, block = enc_ref.shape
    units = down_ref.shape[2]
    base = block * width // 128 + 2 * units * (-(-block // 128))
    for k, late in enumerate((w0, w1, w2, w3)):
        w = late.get()
        enc_ref[k] = get_wide(w, 0, block, width).T
        down_ref[k] = get_wide(w, base, units, block).T


def turn_second_kernel(w0, w1, w2, w3, dec_ref):
    _, n, block = dec_ref.shape
    for k, late in enumerate((w0, w1, w2, w3)):
        dec_ref[k] = get_wide(late.get(), 0, block, n).T


def encode_kernel(
    t_ref, mask_ref, bias_ref, g_late, w_late,
    n0, n1, n2, n3, codes_ref, slope_ref, x_ref,
):
    g_ref = g_late.get()
    feats, _, lanes = g_ref.shape
    height = 2 * lanes
    block = n0.shape[0]
    strip = 4 * block // feats
    depth = feats * strip
    width = codes_ref.shape[0]
    gains = g_ref[:, strip, :].astype(F32).T
    total = jnp.zeros((8, height), F32)
    for f in range(feats):
        x = jnp.concatenate(
            [g_ref[f, pl.ds(0, strip), :], g_ref[f, pl.ds(PITCH, strip), :]], axis=1
        ).astype(F32)
        square = x * x
        for r in range(0, strip - 7, 8):
            total = total + square[r : r + 8]
        tail = square[strip // 8 * 8 :]
        total = total + jnp.concatenate([tail, jnp.zeros_like(tail)], axis=0)
        x_ref[pl.ds(f * strip, strip), :] = x * gains[:strip, f : f + 1]
    total = jnp.sum(total, axis=0, keepdims=True)
    scale = lax.rsqrt(total / depth + 1e-06)
    t = t_ref[0]
    sums = 0.0
    w_ref = w_late.get()
    for k, n_ref in enumerate((n0, n1, n2, n3)):
        at = pl.ds(pl.multiple_of(jnp.bitwise_xor(t, k) * block, 64), block)
        n = (x_ref[at, :] * scale).astype(BF)
        n_ref[...] = n
        sums += dot(w_ref[k], n)
    bias = jnp.broadcast_to(bias_ref[...], (128, width)).T
    factor = 1.0 / math.sqrt(4 * height)
    for j in range(width // TILE):
        for i in range(height // TBLK):
            keep = mask_ref[i, j].astype(F32)
            r, c = slice(j * TILE, (j + 1) * TILE), slice(i * TBLK, (i + 1) * TBLK)
            part = jnp.maximum(sums[r, c] + bias[r, :], 0.0)
            codes_ref[r, c] = (part * part * keep).astype(BF)
            slope_ref[r, c] = part * (keep * (2.0 * factor))


def hidden_kernel(n0, n1, n2, n3, w0, w1, w2, w3, hidden_ref):
    units = hidden_ref.shape[0]
    gate = up = 0.0
    for late, w in ((n0, w0), (n1, w1), (n2, w2), (n3, w3)):
        n, w_ref = late.get()[...], w.get()
        block = n.shape[0]
        gate += dot(get_wide(w_ref, 0, units, block), n)
        up += dot(get_wide(w_ref, units * (-(-block // 128)), units, block), n)
    hidden_ref[...] = (jax.nn.gelu(gate, approximate=True) * up).astype(BF)


def decode_kernel(
    t_ref, codes_ref, before_ref, shifted_ref, hidden_ref, d_late, w0, w1, w2, w3, o_ref, both_ref
):
    t, layer = t_ref[0], t_ref[1]
    n = codes_ref.shape[0]
    block = o_ref.shape[2]
    both_ref[:n] = codes_ref[...]

    @pl.when(layer == 0)
    def _():
        both_ref[n:] = before_ref[...]

    @pl.when(layer != 0)
    def _():
        both_ref[n:] = shifted_ref[...]

    both, hidden = both_ref[...], hidden_ref[...]
    down_ref = d_late.get()
    lanes = o_ref.shape[3]
    for k, late in enumerate((w0, w1, w2, w3)):
        w = late.get()
        value = dot(get_wide(w, 0, block, 2 * n), both) - dot(down_ref[k], hidden)
        spot = jnp.bitwise_xor(t, k)
        for h in range(2):
            o_ref[spot, h] = value[:, h * lanes : (h + 1) * lanes].astype(BF)


def copies_kernel(x_ref, o_ref):
    o_ref[...] = jnp.broadcast_to(x_ref[...][None], o_ref.shape)


def back_kernel(t_ref, e_late, w_late, own_ref, prev_ref):
    t = t_ref[0]
    e_ref, w_ref = e_late.get(), w_late.get()
    n = own_ref.shape[0]
    total = 0.0
    for k in range(4):
        spot = jnp.bitwise_xor(t, k)
        err = jnp.concatenate([e_ref[spot, h] for h in range(2)], axis=1)
        total += dot(w_ref[k], err)
    own_ref[...] = total[:n]
    prev_ref[...] = total[n:].astype(BF)


def decoder_grads_kernel(t_ref, e_ref, c0, c1, c2, c3, own_ref, prev_ref):
    t = t_ref[0]
    n = own_ref.shape[1]
    factor = 1.0 / math.sqrt(8 * e_ref.shape[3])
    total = 0.0
    for k, c in enumerate((c0, c1, c2, c3)):
        spot = jnp.bitwise_xor(t, k)
        err = jnp.concatenate([e_ref[spot, h] for h in range(2)], axis=1)
        total += dot(err, c[...], 1, 1)
    own_ref[...] = total[:, :n] * factor
    prev_ref[...] = total[:, n:] * factor


def encoder_grads_kernel(n0, n1, n2, n3, p0, p1, p2, p3, grad_ref, bias_ref):
    total = bias = 0.0
    ones = jnp.ones((8, p0.shape[1]), BF)
    for n, p in ((n0, p0), (n1, p1), (n2, p2), (n3, p3)):
        total += dot(n[...], p[...], 1, 1)
        bias += dot(ones, p[...], 1, 1)
    grad_ref[...] = total
    bias_ref[...] = bias[:1]


def local(
    resid,
    norm_gain,
    prev_codes,
    feature_mask,
    w_gate,
    w_up,
    w_down,
    enc_weight,
    enc_bias,
    dec_own,
    dec_prev,
):
    height, strip = resid.shape[1:]
    peers = lax.axis_size("feat")
    width = enc_weight.shape[2]
    units = w_gate.shape[2]
    block = strip * peers // 4
    spans = -(-block // 128)
    t = 2 * lax.axis_index("tok_0") + lax.axis_index("tok_1")
    place = jnp.stack([t, lax.axis_index("layer")]).astype(jnp.int32)
    flip = lambda a: jnp.swapaxes(a[0], 0, 1)

    (copies,) = call(
        spread_kernel, (flip(resid), norm_gain), [((peers, 2 * PITCH, height // 2), BF)]
    )
    gathered = exchange(copies)
    first, before = call(
        pack_turn_kernel,
        (enc_weight[0], flip(w_gate), flip(w_up), w_down[0], prev_codes),
        [
            ((block * width // 128 + 3 * units * spans, 128), BF),
            ((width, height), BF),
        ],
    )
    first = gather4(first)
    (own_second,) = call(
        pack_kernel,
        (flip(dec_own), flip(dec_prev)),
        [((2 * block * width // 128, 128), BF)],
        after=(before,),
    )
    far_second = toward(own_second, 2)
    near_second = toward(own_second, 1)
    enc_turned, down_turned = call(
        turn_first_kernel,
        (),
        [((4, width, block), BF), ((4, block, units), BF)],
        late=[Late(w) for w in first],
    )
    cutoff = block * width // 128
    *normed, codes, slope = call(
        encode_kernel,
        (place, feature_mask[0], enc_bias),
        [((block, height), BF)] * 4 + [((width, height), BF), ((width, height), F32)],
        [pltpu.VMEM((4 * block, height), F32)],
        late=(Late(gathered), Late(enc_turned)),
    )
    shifted = lax.ppermute(codes, "layer", [(0, 1)])
    hidden, far_second = call(
        hidden_kernel,
        (),
        [((units, height), BF)],
        late=(*(Late(n) for n in normed), *(Late(w, cutoff, cutoff + 2 * units * spans) for w in first)),
        through=(far_second,),
    )
    second = [own_second, near_second, far_second, toward(far_second, 1)]
    (dec_turned,) = call(
        turn_second_kernel, (), [((4, 2 * width, block), BF)], late=[Late(w) for w in second]
    )
    parts, both = call(
        decode_kernel,
        (place, codes, before, shifted, hidden),
        [((4, 2, block, height // 2), BF), ((2 * width, height), BF)],
        late=(Late(down_turned), *(Late(w) for w in second)),
    )
    arrived = exchange(parts.reshape(peers, ROWS, height // 2))
    total = jnp.sum(arrived.astype(F32), axis=0).astype(BF)
    normed = exchange4(normed)
    (copies,) = call(
        copies_kernel, (total,), [(arrived.shape, BF)], after=(dec_turned, *normed[1:])
    )
    errors = exchange(copies).reshape(parts.shape)
    both = gather4(both)
    own_back, prev_back = call(
        back_kernel,
        (place,),
        [((width, height), F32), ((width, height), BF)],
        late=(Late(errors), Late(dec_turned)),
        after=both[1:],
    )
    err = exchange(errors, TOK)
    later = lax.ppermute(prev_back, "layer", [(1, 0)]).astype(F32)
    pregrad = gather4(((own_back + later) * slope).astype(BF))
    grad_own, grad_prev = call(
        decoder_grads_kernel, (place, err, *both), [((block, width), F32)] * 2
    )
    grad_enc, grad_bias = call(
        encoder_grads_kernel,
        (*normed, *pregrad),
        [((block, width), F32), ((1, width), F32)],
    )
    return (grad_enc[None], grad_bias, grad_own.T[None], grad_prev.T[None])


def solution(mesh):
    split = Mesh(
        mesh.devices.reshape(mesh.shape["layer"], mesh.shape["feat"], 2, 2),
        ("layer", "feat", "tok_0", "tok_1"),
    )
    placed = (
        P("layer", TOK, "feat"),
        P("layer", "feat"),
        P(TOK, "feat"),
        P("layer", TOK, "feat"),
        P("layer", TOK, "feat"),
        P("layer", TOK, "feat"),
        P("layer", "feat", TOK),
        P("layer", TOK, "feat"),
        P("layer", "feat"),
        P("layer", "feat", TOK),
        P("layer", "feat", TOK),
    )
    return jax.shard_map(
        local,
        mesh=split,
        in_specs=placed,
        out_specs=(
            P("layer", TOK, "feat"),
            P("layer", "feat"),
            P("layer", "feat", TOK),
            P("layer", "feat", TOK),
        ),
        check_vma=False,
    )
```

```python
import math

import jax
import jax.numpy as jnp
from jax import lax
from jax.experimental import pallas as pl
from jax.experimental.pallas import tpu as pltpu
from jax.sharding import Mesh
from jax.sharding import PartitionSpec as P

TILE = 128
TBLK = 128
BF = jnp.bfloat16
F32 = jnp.float32
TOK = ("tok_0", "tok_1")
PARAMS = pltpu.CompilerParams(vmem_limit_bytes=24 * 1024 * 1024)
VM = pl.BlockSpec(memory_space=pltpu.VMEM)
SM = pl.BlockSpec(memory_space=pltpu.SMEM)


ANY = pl.BlockSpec(memory_space=pl.ANY)
PITCH = 40
ROWS = 72


def call(kernel, ins, outs, after=(), through=(), scratch=(), leaving=(), plain=False):
    def held(a):
        small = plain or a.dtype == jnp.int32 or a.size < 2**15
        return a if small else pltpu.with_memory_space_constraint(a, pltpu.VMEM)

    n, p, skip = len(outs), len(through), len(ins) + len(after)
    specs = [SM if a.dtype == jnp.int32 else VM for a in ins]

    def body(*refs):
        rest = refs[skip + p :]
        kernel(*refs[: len(ins)], *rest[:n], *rest[n + p :])

    return pl.pallas_call(
        body,
        out_shape=[
            (pltpu.HBM if i in leaving else pltpu.VMEM)(*o) for i, o in enumerate(outs)
        ]
        + [pltpu.VMEM(a.shape, a.dtype) for a in through],
        in_specs=specs + [VM] * (skip - len(ins) + p),
        out_specs=[VM] * (n + p),
        input_output_aliases={skip + i: n + i for i in range(p)},
        scratch_shapes=list(scratch),
        compiler_params=PARAMS,
        name=kernel.__name__,
    )(*(held(a) for a in (*ins, *after, *through)))


def corner(arrays):
    return sum(lax.slice(a, (0, 0), (8, 128)).astype(F32) for a in arrays)


def dot(a, b, ca=1, cb=0):
    return lax.dot_general(a, b, (((ca,), (cb,)), ((), ())), preferred_element_type=F32)


def toward(x, k):
    return lax.ppermute(x, TOK, [(i, i ^ k) for i in range(4)])


def gather4(x):
    far = toward(x, 2)
    return [x, toward(x, 1), far, toward(far, 1)]


def exchange4(blocks):
    return [blocks[0]] + [toward(blocks[k], k) for k in (1, 2, 3)]


def exchange(blocks):
    return lax.all_to_all(blocks, "feat", split_axis=0, concat_axis=0, tiled=True)


def spread_kernel(x_ref, gain_ref, o_ref):
    strip, height = x_ref.shape
    lanes = height // 2
    x = x_ref[...].astype(F32)
    gain = gain_ref[...].astype(F32)
    row = jnp.concatenate([gain, jnp.zeros((1, lanes - strip), F32)], axis=1)
    rest = jnp.zeros((PITCH - strip - 1, lanes), F32)
    parts = [x[:, :lanes], row, rest, x[:, lanes:], row, rest]
    o_ref[...] = jnp.broadcast_to(jnp.concatenate(parts, axis=0).astype(BF)[None], o_ref.shape)


def put_wide(o_ref, at, w):
    rows, cols = w.shape
    for c in range(0, cols, 128):
        wide = min(128, cols - c)
        o_ref[pl.ds(at, rows), pl.ds(0, wide)] = w[:, c : c + wide]
        at += rows
    return at


def get_wide(w_ref, at, rows, cols):
    pieces = [
        w_ref[pl.ds(at + rows * i, rows), : min(128, cols - 128 * i)] for i in range(-(-cols // 128))
    ]
    return jnp.concatenate(pieces, axis=1)


def pack_kernel(*refs):
    *ws, o_ref = refs
    at = 0
    for w in ws:
        at = put_wide(o_ref, at, w[...])


def pack_turn_kernel(*refs):
    *ws, x_ref, o_ref, turned_ref = refs
    pack_kernel(*ws, o_ref)
    turned_ref[...] = x_ref[...].astype(F32).T.astype(BF)


def pin_kernel(*refs):
    pass


def pregrad_kernel(own_ref, later_ref, slope_ref, o_ref):
    back = own_ref[...] + later_ref[...].astype(F32)
    o_ref[...] = (back * slope_ref[...]).astype(BF)


def encode_kernel(
    t_ref, mask_ref, g_ref, w0, w1, w2, w3, bias_ref,
    n0, n1, n2, n3, codes_ref, slope_ref, hidden_ref, x_ref,
):
    feats, _, lanes = g_ref.shape
    height = 2 * lanes
    block = n0.shape[0]
    strip = 4 * block // feats
    depth = feats * strip
    width = codes_ref.shape[0]
    units = hidden_ref.shape[0]
    gains = g_ref[:, strip, :].astype(F32).T
    total = jnp.zeros((8, height), F32)
    for f in range(feats):
        x = jnp.concatenate(
            [g_ref[f, pl.ds(0, strip), :], g_ref[f, pl.ds(PITCH, strip), :]], axis=1
        ).astype(F32)
        square = x * x
        for r in range(0, strip - 7, 8):
            total = total + square[r : r + 8]
        tail = square[strip // 8 * 8 :]
        total = total + jnp.concatenate([tail, jnp.zeros_like(tail)], axis=0)
        x_ref[pl.ds(f * strip, strip), :] = x * gains[:strip, f : f + 1]
    total = jnp.sum(total, axis=0, keepdims=True)
    scale = lax.rsqrt(total / depth + 1e-06)
    t = t_ref[0]
    sums = gate = up = 0.0
    for k, (n_ref, w) in enumerate(((n0, w0), (n1, w1), (n2, w2), (n3, w3))):
        at = pl.ds(pl.multiple_of(jnp.bitwise_xor(t, k) * block, 64), block)
        n = (x_ref[at, :] * scale).astype(BF)
        n_ref[...] = n
        sums += dot(get_wide(w, 0, block, width), n, 0, 0)
        base = block * width // 128
        gate += dot(get_wide(w, base, units, block), n)
        up += dot(get_wide(w, base + units * (-(-block // 128)), units, block), n)
    bias = jnp.broadcast_to(bias_ref[...], (128, width)).T
    factor = 1.0 / math.sqrt(4 * height)
    for j in range(width // TILE):
        for i in range(height // TBLK):
            keep = mask_ref[i, j].astype(F32)
            r, c = slice(j * TILE, (j + 1) * TILE), slice(i * TBLK, (i + 1) * TBLK)
            part = jnp.maximum(sums[r, c] + bias[r, :], 0.0)
            codes_ref[r, c] = (part * part * keep).astype(BF)
            slope_ref[r, c] = part * (keep * (2.0 * factor))
    hidden_ref[...] = (jax.nn.gelu(gate, approximate=True) * up).astype(BF)


def decode_kernel(
    t_ref, codes_ref, before_ref, shifted_ref, hidden_ref, w0, w1, w2, w3, o_ref, both_ref
):
    t, layer = t_ref[0], t_ref[1]
    n = codes_ref.shape[0]
    units = hidden_ref.shape[0]
    block = o_ref.shape[0] * ROWS // 8
    both_ref[:n] = codes_ref[...]

    @pl.when(layer == 0)
    def _():
        both_ref[n:] = before_ref[...]

    @pl.when(layer != 0)
    def _():
        both_ref[n:] = shifted_ref[...]

    both, hidden = both_ref[...], hidden_ref[...]
    peers, rows, lanes = o_ref.shape
    each = block // rows
    for k, w in enumerate((w0, w1, w2, w3)):
        decoder = jnp.concatenate(
            [get_wide(w, 0, block, n), get_wide(w, block * n // 128, block, n)], axis=1
        )
        down = get_wide(w, 2 * block * n // 128, units, block)
        value = dot(decoder, both) - dot(down, hidden, 0, 0)
        spot = jnp.bitwise_xor(t, k) * each
        for i in range(each):
            for h in range(2):
                o_ref[spot + (h * peers // 2 + i)] = value[
                    i * rows : (i + 1) * rows, h * lanes : (h + 1) * lanes
                ].astype(BF)


def total_kernel(x_ref, o_ref):
    total = jnp.sum(x_ref[...].astype(F32), axis=0).astype(BF)
    o_ref[...] = jnp.broadcast_to(total[None], o_ref.shape)


def back_kernel(t_ref, e_ref, w0, w1, w2, w3, own_ref, prev_ref, e0, e1, e2, e3):
    t = t_ref[0]
    peers, rows, lanes = e_ref.shape
    n = own_ref.shape[0]
    block = e0.shape[0]
    each = block // rows
    total = 0.0
    for k, (err_ref, w) in enumerate(((e0, w0), (e1, w1), (e2, w2), (e3, w3))):
        spot = jnp.bitwise_xor(t, k) * each
        half = [
            jnp.concatenate(
                [e_ref[spot + (h * peers // 2 + i)].astype(F32) for i in range(each)], axis=0
            ).astype(BF)
            for h in range(2)
        ]
        err = jnp.concatenate(half, axis=1)
        err_ref[...] = err
        decoder = jnp.concatenate(
            [get_wide(w, 0, block, n), get_wide(w, block * n // 128, block, n)], axis=1
        )
        total += dot(decoder, err, 0, 0)
    own_ref[...] = total[:n]
    prev_ref[...] = total[n:].astype(BF)


def decoder_grads_kernel(e0, e1, e2, e3, c0, c1, c2, c3, own_ref, prev_ref):
    n = own_ref.shape[1]
    factor = 1.0 / math.sqrt(4 * e0.shape[1])
    total = 0.0
    for e, c in ((e0, c0), (e1, c1), (e2, c2), (e3, c3)):
        total += dot(e[...], c[...], 1, 1)
    own_ref[...] = total[:, :n] * factor
    prev_ref[...] = total[:, n:] * factor


def encoder_grads_kernel(n0, n1, n2, n3, p0, p1, p2, p3, grad_ref, bias_ref):
    total = bias = 0.0
    ones = jnp.ones((8, p0.shape[1]), BF)
    for n, p in ((n0, p0), (n1, p1), (n2, p2), (n3, p3)):
        total += dot(n[...], p[...], 1, 1)
        bias += dot(ones, p[...], 1, 1)
    grad_ref[...] = total
    bias_ref[...] = bias[:1]


def local(
    resid,
    norm_gain,
    prev_codes,
    feature_mask,
    w_gate,
    w_up,
    w_down,
    enc_weight,
    enc_bias,
    dec_own,
    dec_prev,
):
    height, strip = resid.shape[1:]
    peers = lax.axis_size("feat")
    width = enc_weight.shape[2]
    units = w_gate.shape[2]
    block = strip * peers // 4
    spans = -(-block // 128)
    t = 2 * lax.axis_index("tok_0") + lax.axis_index("tok_1")
    place = jnp.stack([t, lax.axis_index("layer")]).astype(jnp.int32)
    flip = lambda a: jnp.swapaxes(a[0], 0, 1)

    (copies,) = call(
        spread_kernel,
        (flip(resid), norm_gain),
        [((peers, 2 * PITCH, height // 2), BF)],
        leaving=(0,),
        plain=True,
    )
    gathered = exchange(copies)
    (second,) = call(
        pack_kernel,
        (flip(dec_own), flip(dec_prev), w_down[0]),
        [((2 * block * width // 128 + units * spans, 128), BF)],
        plain=True,
    )
    near, far = toward(second, 1), toward(second, 2)
    first, before = call(
        pack_turn_kernel,
        (enc_weight[0], flip(w_gate), flip(w_up), prev_codes),
        [((block * width // 128 + 2 * units * spans, 128), BF), ((width, height), BF)],
        plain=True,
    )
    first = gather4(first)
    *normed, codes, slope, hidden = call(
        encode_kernel,
        (place, feature_mask[0], gathered, *first, enc_bias),
        [((block, height), BF)] * 4
        + [((width, height), BF), ((width, height), F32), ((units, height), BF)],
        scratch=[pltpu.VMEM((4 * block, height), F32)],
    )
    shifted = lax.ppermute(codes, "layer", [(0, 1)])
    (far,) = call(pin_kernel, (), [], after=(slope,), through=(far,))
    second = [second, near, far, toward(far, 1)]
    parts, both = call(
        decode_kernel,
        (place, codes, before, shifted, hidden, *second),
        [((peers, ROWS, height // 2), BF), ((2 * width, height), BF)],
        leaving=(0,),
    )
    arrived = exchange(parts)
    normed = exchange4(normed)
    (copies,) = call(total_kernel, (arrived,), [(parts.shape, BF)], after=(corner(normed[1:]),), leaving=(0,))
    errors = exchange(copies)
    both = gather4(both)
    own_back, prev_back, *err = call(
        back_kernel,
        (place, errors, *second),
        [((width, height), F32), ((width, height), BF)] + [((block, height), BF)] * 4,
        after=(corner(both[1:]),),
    )
    later = lax.ppermute(prev_back, "layer", [(1, 0)])
    (pregrad,) = call(
        pregrad_kernel, (own_back, later, slope), [((width, height), BF)]
    )
    pregrad = gather4(pregrad)
    err[1], err[3] = call(
        pin_kernel, (), [], after=(pregrad[2],), through=(err[1], err[3])
    )
    err = exchange4(err)
    grad_own, grad_prev = call(
        decoder_grads_kernel, (*err, *both), [((block, width), F32)] * 2, leaving=(0, 1)
    )
    grad_enc, grad_bias = call(
        encoder_grads_kernel,
        (*normed, *pregrad),
        [((block, width), F32), ((1, width), F32)],
        leaving=(0, 1),
    )
    return (grad_enc[None], grad_bias, grad_own.T[None], grad_prev.T[None])


def solution(mesh):
    split = Mesh(
        mesh.devices.reshape(mesh.shape["layer"], mesh.shape["feat"], 2, 2),
        ("layer", "feat", "tok_0", "tok_1"),
    )
    placed = (
        P("layer", TOK, "feat"),
        P("layer", "feat"),
        P(TOK, "feat"),
        P("layer", TOK, "feat"),
        P("layer", TOK, "feat"),
        P("layer", TOK, "feat"),
        P("layer", "feat", TOK),
        P("layer", TOK, "feat"),
        P("layer", "feat"),
        P("layer", "feat", TOK),
        P("layer", "feat", TOK),
    )
    return jax.shard_map(
        local,
        mesh=split,
        in_specs=placed,
        out_specs=(
            P("layer", TOK, "feat"),
            P("layer", "feat"),
            P("layer", "feat", TOK),
            P("layer", "feat", TOK),
        ),
        check_vma=False,
    )
```

```python
import math

import jax
import jax.numpy as jnp
from jax import lax
from jax.experimental import pallas as pl
from jax.experimental.pallas import tpu as pltpu
from jax.sharding import Mesh
from jax.sharding import PartitionSpec as P

TILE = 128
TBLK = 128
BF = jnp.bfloat16
F32 = jnp.float32
TOK = ("tok_0", "tok_1")
FEAT = ("y_1", "y_0", "z_1", "z_0")
NEAR = ("y_0", "z_0")
WIDE = ("y_1", "z_1")
PARAMS = pltpu.CompilerParams(vmem_limit_bytes=24 * 1024 * 1024)
VM = pl.BlockSpec(memory_space=pltpu.VMEM)
SM = pl.BlockSpec(memory_space=pltpu.SMEM)


ANY = pl.BlockSpec(memory_space=pl.ANY)
PITCH = 40
ROWS = 72


def call(kernel, ins, outs, after=(), through=(), scratch=(), leaving=(), plain=False):
    def held(a):
        small = plain or a.dtype == jnp.int32 or a.size < 2**15
        return a if small else pltpu.with_memory_space_constraint(a, pltpu.VMEM)

    n, p, skip = len(outs), len(through), len(ins) + len(after)
    specs = [SM if a.dtype == jnp.int32 else VM for a in ins]

    def body(*refs):
        rest = refs[skip + p :]
        kernel(*refs[: len(ins)], *rest[:n], *rest[n + p :])

    return pl.pallas_call(
        body,
        out_shape=[
            (pltpu.HBM if i in leaving else pltpu.VMEM)(*o) for i, o in enumerate(outs)
        ]
        + [pltpu.VMEM(a.shape, a.dtype) for a in through],
        in_specs=specs + [VM] * (skip - len(ins) + p),
        out_specs=[VM] * (n + p),
        input_output_aliases={skip + i: n + i for i in range(p)},
        scratch_shapes=list(scratch),
        compiler_params=PARAMS,
        name=kernel.__name__,
    )(*(held(a) for a in (*ins, *after, *through)))


def corner(arrays):
    return sum(lax.slice(a, (0, 0), (8, 128)).astype(F32) for a in arrays)


def dot(a, b, ca=1, cb=0):
    return lax.dot_general(a, b, (((ca,), (cb,)), ((), ())), preferred_element_type=F32)


def toward(x, k, axes=TOK):
    return lax.ppermute(x, axes, [(i, i ^ k) for i in range(4)])


def gather4(x):
    far = toward(x, 2)
    return [x, toward(x, 1), far, toward(far, 1)]


def exchange4(blocks, axes=TOK):
    return [blocks[0]] + [toward(blocks[k], k, axes) for k in (1, 2, 3)]


def exchange(blocks, axes=FEAT):
    return lax.all_to_all(blocks, axes, split_axis=0, concat_axis=0, tiled=True)


def spread_kernel(x_ref, gain_ref, o_ref):
    strip, height = x_ref.shape
    lanes = height // 2
    x = x_ref[...].astype(F32)
    gain = gain_ref[...].astype(F32)
    row = jnp.concatenate([gain, jnp.zeros((1, lanes - strip), F32)], axis=1)
    rest = jnp.zeros((PITCH - strip - 1, lanes), F32)
    parts = [x[:, :lanes], row, rest, x[:, lanes:], row, rest]
    o_ref[...] = jnp.broadcast_to(jnp.concatenate(parts, axis=0).astype(BF)[None], o_ref.shape)


def put_wide(o_ref, at, w):
    rows, cols = w.shape
    for c in range(0, cols, 128):
        wide = min(128, cols - c)
        o_ref[pl.ds(at, rows), pl.ds(0, wide)] = w[:, c : c + wide]
        at += rows
    return at


def get_wide(w_ref, at, rows, cols):
    pieces = [
        w_ref[pl.ds(at + rows * i, rows), : min(128, cols - 128 * i)] for i in range(-(-cols // 128))
    ]
    return jnp.concatenate(pieces, axis=1)


def pack_kernel(*refs):
    *ws, o_ref = refs
    at = 0
    for w in ws:
        at = put_wide(o_ref, at, w[...])


def pack_turn_kernel(*refs):
    *ws, x_ref, o_ref, turned_ref = refs
    pack_kernel(*ws, o_ref)
    turned_ref[...] = x_ref[...].astype(F32).T.astype(BF)


def pin_kernel(*refs):
    pass


def pregrad_kernel(own_ref, later_ref, slope_ref, o_ref):
    back = own_ref[...] + later_ref[...].astype(F32)
    o_ref[...] = (back * slope_ref[...]).astype(BF)


def encode_kernel(
    t_ref, mask_ref, g_ref, w0, w1, w2, w3, bias_ref,
    n0, n1, n2, n3, codes_ref, slope_ref, hidden_ref, x_ref,
):
    feats, _, lanes = g_ref.shape
    height = 2 * lanes
    block = n0.shape[0]
    strip = 4 * block // feats
    depth = feats * strip
    width = codes_ref.shape[0]
    units = hidden_ref.shape[0]
    gains = g_ref[:, strip, :].astype(F32).T
    total = jnp.zeros((8, height), F32)
    for f in range(feats):
        x = jnp.concatenate(
            [g_ref[f, pl.ds(0, strip), :], g_ref[f, pl.ds(PITCH, strip), :]], axis=1
        ).astype(F32)
        square = x * x
        for r in range(0, strip - 7, 8):
            total = total + square[r : r + 8]
        tail = square[strip // 8 * 8 :]
        total = total + jnp.concatenate([tail, jnp.zeros_like(tail)], axis=0)
        x_ref[pl.ds(f * strip, strip), :] = x * gains[:strip, f : f + 1]
    total = jnp.sum(total, axis=0, keepdims=True)
    scale = lax.rsqrt(total / depth + 1e-06)
    t = t_ref[0]
    sums = gate = up = 0.0
    for k, (n_ref, w) in enumerate(((n0, w0), (n1, w1), (n2, w2), (n3, w3))):
        at = pl.ds(pl.multiple_of(jnp.bitwise_xor(t, k) * block, 64), block)
        n = (x_ref[at, :] * scale).astype(BF)
        n_ref[...] = n
        sums += dot(get_wide(w, 0, block, width), n, 0, 0)
        base = block * width // 128
        gate += dot(get_wide(w, base, units, block), n)
        up += dot(get_wide(w, base + units * (-(-block // 128)), units, block), n)
    bias = jnp.broadcast_to(bias_ref[...], (128, width)).T
    factor = 1.0 / math.sqrt(4 * height)
    for j in range(width // TILE):
        for i in range(height // TBLK):
            keep = mask_ref[i, j].astype(F32)
            r, c = slice(j * TILE, (j + 1) * TILE), slice(i * TBLK, (i + 1) * TBLK)
            part = jnp.maximum(sums[r, c] + bias[r, :], 0.0)
            codes_ref[r, c] = (part * part * keep).astype(BF)
            slope_ref[r, c] = part * (keep * (2.0 * factor))
    hidden_ref[...] = (jax.nn.gelu(gate, approximate=True) * up).astype(BF)


def decode_kernel(
    t_ref, codes_ref, before_ref, shifted_ref, hidden_ref, w0, w1, w2, w3,
    o0, o1, o2, o3, both_ref, s_ref,
):
    t, layer, near = t_ref[0], t_ref[1], t_ref[2]
    n = codes_ref.shape[0]
    units = hidden_ref.shape[0]
    _, block, lanes = o0.shape
    both_ref[:n] = codes_ref[...]

    @pl.when(layer == 0)
    def _():
        both_ref[n:] = before_ref[...]

    @pl.when(layer != 0)
    def _():
        both_ref[n:] = shifted_ref[...]

    both, hidden = both_ref[...], hidden_ref[...]
    for k, w in enumerate((w0, w1, w2, w3)):
        decoder = jnp.concatenate(
            [get_wide(w, 0, block, n), get_wide(w, block * n // 128, block, n)], axis=1
        )
        down = get_wide(w, 2 * block * n // 128, units, block)
        value = dot(decoder, both) - dot(down, hidden, 0, 0)
        spot = jnp.bitwise_xor(jnp.bitwise_xor(t, near), k)
        for h in range(2):
            s_ref[spot, h] = value[:, h * lanes : (h + 1) * lanes].astype(BF)
    for m, o_ref in enumerate((o0, o1, o2, o3)):
        o_ref[...] = s_ref[m]


def near_total_kernel(x0, x1, x2, x3, o_ref):
    o_ref[...] = sum(x[...].astype(F32) for x in (x0, x1, x2, x3)).astype(BF)


def total_kernel(x_ref, o_ref):
    total = jnp.sum(x_ref[...].astype(F32), axis=0).astype(BF)
    o_ref[...] = jnp.broadcast_to(total[None], o_ref.shape)


def back_kernel(
    t_ref, x0, x1, x2, x3, w0, w1, w2, w3, own_ref, prev_ref, e0, e1, e2, e3, s_ref
):
    t, near = t_ref[0], t_ref[2]
    for m, x in enumerate((x0, x1, x2, x3)):
        s_ref[jnp.bitwise_xor(near, m)] = x[...]
    n = own_ref.shape[0]
    block = e0.shape[0]
    total = 0.0
    for k, (err_ref, w) in enumerate(((e0, w0), (e1, w1), (e2, w2), (e3, w3))):
        spot = jnp.bitwise_xor(t, k)
        err = jnp.concatenate([s_ref[spot, h] for h in range(2)], axis=1)
        err_ref[...] = err
        decoder = jnp.concatenate(
            [get_wide(w, 0, block, n), get_wide(w, block * n // 128, block, n)], axis=1
        )
        total += dot(decoder, err, 0, 0)
    own_ref[...] = total[:n]
    prev_ref[...] = total[n:].astype(BF)


def decoder_grads_kernel(e0, e1, e2, e3, c0, c1, c2, c3, own_ref, prev_ref):
    n = own_ref.shape[1]
    factor = 1.0 / math.sqrt(4 * e0.shape[1])
    total = 0.0
    for e, c in ((e0, c0), (e1, c1), (e2, c2), (e3, c3)):
        total += dot(e[...], c[...], 1, 1)
    own_ref[...] = total[:, :n] * factor
    prev_ref[...] = total[:, n:] * factor


def encoder_grads_kernel(n0, n1, n2, n3, p0, p1, p2, p3, grad_ref, bias_ref):
    total = bias = 0.0
    ones = jnp.ones((8, p0.shape[1]), BF)
    for n, p in ((n0, p0), (n1, p1), (n2, p2), (n3, p3)):
        total += dot(n[...], p[...], 1, 1)
        bias += dot(ones, p[...], 1, 1)
    grad_ref[...] = total
    bias_ref[...] = bias[:1]


def local(
    resid,
    norm_gain,
    prev_codes,
    feature_mask,
    w_gate,
    w_up,
    w_down,
    enc_weight,
    enc_bias,
    dec_own,
    dec_prev,
):
    height, strip = resid.shape[1:]
    peers = lax.axis_size(FEAT)
    width = enc_weight.shape[2]
    units = w_gate.shape[2]
    block = strip * peers // 4
    spans = -(-block // 128)
    t = 2 * lax.axis_index("tok_0") + lax.axis_index("tok_1")
    near = 2 * lax.axis_index("y_0") + lax.axis_index("z_0")
    place = jnp.stack([t, lax.axis_index("layer"), near]).astype(jnp.int32)
    flip = lambda a: jnp.swapaxes(a[0], 0, 1)

    (copies,) = call(
        spread_kernel,
        (flip(resid), norm_gain),
        [((peers, 2 * PITCH, height // 2), BF)],
        leaving=(0,),
        plain=True,
    )
    gathered = exchange(copies)
    (second,) = call(
        pack_kernel,
        (flip(dec_own), flip(dec_prev), w_down[0]),
        [((2 * block * width // 128 + units * spans, 128), BF)],
        plain=True,
    )
    beside, far = toward(second, 1), toward(second, 2)
    first, before = call(
        pack_turn_kernel,
        (enc_weight[0], flip(w_gate), flip(w_up), prev_codes),
        [((block * width // 128 + 2 * units * spans, 128), BF), ((width, height), BF)],
        plain=True,
    )
    first = gather4(first)
    *normed, codes, slope, hidden = call(
        encode_kernel,
        (place, feature_mask[0], gathered, *first, enc_bias),
        [((block, height), BF)] * 4
        + [((width, height), BF), ((width, height), F32), ((units, height), BF)],
        scratch=[pltpu.VMEM((4 * block, height), F32)],
    )
    shifted = lax.ppermute(codes, "layer", [(0, 1)])
    (far,) = call(pin_kernel, (), [], after=(slope,), through=(far,))
    second = [second, beside, far, toward(far, 1)]
    slab = (2, block, height // 2)
    *parts, both = call(
        decode_kernel,
        (place, codes, before, shifted, hidden, *second),
        [(slab, BF)] * 4 + [((2 * width, height), BF)],
        scratch=[pltpu.VMEM((4, *slab), BF)],
    )
    (part,) = call(near_total_kernel, exchange4(parts, NEAR), [(slab, BF)], leaving=(0,))
    arrived = exchange(part.reshape(peers // 4, ROWS, height // 2), WIDE)
    normed = exchange4(normed)
    (copies,) = call(
        total_kernel,
        (arrived,),
        [(arrived.shape, BF)],
        after=(corner(normed[1:]),),
        leaving=(0,),
    )
    errors = exchange(copies, WIDE).reshape(slab)
    both = gather4(both)
    errors = exchange4([errors] * 4, NEAR)
    own_back, prev_back, *err = call(
        back_kernel,
        (place, *errors, *second),
        [((width, height), F32), ((width, height), BF)] + [((block, height), BF)] * 4,
        after=(corner(both[1:]),),
        scratch=[pltpu.VMEM((4, *slab), BF)],
    )
    later = lax.ppermute(prev_back, "layer", [(1, 0)])
    (pregrad,) = call(
        pregrad_kernel, (own_back, later, slope), [((width, height), BF)]
    )
    pregrad = gather4(pregrad)
    err[1], err[3] = call(
        pin_kernel, (), [], after=(pregrad[2],), through=(err[1], err[3])
    )
    err = exchange4(err)
    grad_own, grad_prev = call(
        decoder_grads_kernel, (*err, *both), [((block, width), F32)] * 2, leaving=(0, 1)
    )
    grad_enc, grad_bias = call(
        encoder_grads_kernel,
        (*normed, *pregrad),
        [((block, width), F32), ((1, width), F32)],
        leaving=(0, 1),
    )
    return (grad_enc[None], grad_bias, grad_own.T[None], grad_prev.T[None])


def solution(mesh):
    split = Mesh(
        mesh.devices.reshape(mesh.shape["layer"], 4, 2, 4, 2, 2, 2),
        ("layer", *FEAT, *TOK),
    )
    placed = (
        P("layer", TOK, FEAT),
        P("layer", FEAT),
        P(TOK, FEAT),
        P("layer", TOK, FEAT),
        P("layer", TOK, FEAT),
        P("layer", TOK, FEAT),
        P("layer", FEAT, TOK),
        P("layer", TOK, FEAT),
        P("layer", FEAT),
        P("layer", FEAT, TOK),
        P("layer", FEAT, TOK),
    )
    return jax.shard_map(
        local,
        mesh=split,
        in_specs=placed,
        out_specs=(
            P("layer", TOK, FEAT),
            P("layer", FEAT),
            P("layer", FEAT, TOK),
            P("layer", FEAT, TOK),
        ),
        check_vma=False,
    )
```

```python
import math

import jax
import jax.numpy as jnp
from jax import lax
from jax.experimental import pallas as pl
from jax.experimental.pallas import tpu as pltpu
from jax.sharding import Mesh
from jax.sharding import PartitionSpec as P

TILE = 128
TBLK = 128
BF = jnp.bfloat16
F32 = jnp.float32
TOK = ("tok_0", "tok_1")
PARAMS = pltpu.CompilerParams(vmem_limit_bytes=24 * 1024 * 1024)
VM = pl.BlockSpec(memory_space=pltpu.VMEM)
SM = pl.BlockSpec(memory_space=pltpu.SMEM)


ANY = pl.BlockSpec(memory_space=pl.ANY)
PITCH = 40
ROWS = 72


def call(kernel, ins, outs, after=(), through=(), scratch=(), leaving=(), plain=False):
    def held(a):
        small = plain or a.dtype == jnp.int32 or a.size < 2**15
        return a if small else pltpu.with_memory_space_constraint(a, pltpu.VMEM)

    n, p, skip = len(outs), len(through), len(ins) + len(after)
    specs = [SM if a.dtype == jnp.int32 else VM for a in ins]

    def body(*refs):
        rest = refs[skip + p :]
        kernel(*refs[: len(ins)], *rest[:n], *rest[n + p :])

    return pl.pallas_call(
        body,
        out_shape=[
            (pltpu.HBM if i in leaving else pltpu.VMEM)(*o) for i, o in enumerate(outs)
        ]
        + [pltpu.VMEM(a.shape, a.dtype) for a in through],
        in_specs=specs + [VM] * (skip - len(ins) + p),
        out_specs=[VM] * (n + p),
        input_output_aliases={skip + i: n + i for i in range(p)},
        scratch_shapes=list(scratch),
        compiler_params=PARAMS,
        name=kernel.__name__,
    )(*(held(a) for a in (*ins, *after, *through)))


def corner(arrays):
    return sum(lax.slice(a, (0, 0), (8, 128)).astype(F32) for a in arrays)


def dot(a, b, ca=1, cb=0):
    return lax.dot_general(a, b, (((ca,), (cb,)), ((), ())), preferred_element_type=F32)


def toward(x, k):
    return lax.ppermute(x, TOK, [(i, i ^ k) for i in range(4)])


def gather4(x):
    far = toward(x, 2)
    return [x, toward(x, 1), far, toward(far, 1)]


def exchange4(blocks):
    return [blocks[0]] + [toward(blocks[k], k) for k in (1, 2, 3)]


def exchange(blocks):
    return lax.all_to_all(blocks, "feat", split_axis=0, concat_axis=0, tiled=True)


def spread_kernel(x_ref, gain_ref, o_ref):
    strip, height = x_ref.shape
    lanes = height // 2
    x = x_ref[...].astype(F32)
    gain = gain_ref[...].astype(F32)
    row = jnp.concatenate([gain, jnp.zeros((1, lanes - strip), F32)], axis=1)
    rest = jnp.zeros((PITCH - strip - 1, lanes), F32)
    parts = [x[:, :lanes], row, rest, x[:, lanes:], row, rest]
    o_ref[...] = jnp.broadcast_to(jnp.concatenate(parts, axis=0).astype(BF)[None], o_ref.shape)


def put_wide(o_ref, at, w):
    rows, cols = w.shape
    for c in range(0, cols, 128):
        wide = min(128, cols - c)
        o_ref[pl.ds(at, rows), pl.ds(0, wide)] = w[:, c : c + wide]
        at += rows
    return at


def get_wide(w_ref, at, rows, cols):
    pieces = [
        w_ref[pl.ds(at + rows * i, rows), : min(128, cols - 128 * i)] for i in range(-(-cols // 128))
    ]
    return jnp.concatenate(pieces, axis=1)


def pack_kernel(*refs):
    *ws, o_ref = refs
    at = 0
    for w in ws:
        at = put_wide(o_ref, at, w[...])


def pack_turn_kernel(*refs):
    *ws, x_ref, o_ref, turned_ref = refs
    pack_kernel(*ws, o_ref)
    turned_ref[...] = x_ref[...].astype(F32).T.astype(BF)


def pin_kernel(*refs):
    pass


def pregrad_kernel(own_ref, later_ref, slope_ref, o_ref):
    back = own_ref[...] + later_ref[...].astype(F32)
    o_ref[...] = (back * slope_ref[...]).astype(BF)


def encode_kernel(
    t_ref, mask_ref, g_ref, w0, w1, w2, w3, bias_ref,
    n0, n1, n2, n3, codes_ref, slope_ref, hidden_ref, x_ref,
):
    feats, _, lanes = g_ref.shape
    height = 2 * lanes
    block = n0.shape[0]
    strip = 4 * block // feats
    depth = feats * strip
    width = codes_ref.shape[0]
    units = hidden_ref.shape[0]
    gains = g_ref[:, strip, :].astype(F32).T
    total = jnp.zeros((8, height), F32)
    for f in range(feats):
        x = jnp.concatenate(
            [g_ref[f, pl.ds(0, strip), :], g_ref[f, pl.ds(PITCH, strip), :]], axis=1
        ).astype(F32)
        square = x * x
        for r in range(0, strip - 7, 8):
            total = total + square[r : r + 8]
        tail = square[strip // 8 * 8 :]
        total = total + jnp.concatenate([tail, jnp.zeros_like(tail)], axis=0)
        x_ref[pl.ds(f * strip, strip), :] = x * gains[:strip, f : f + 1]
    total = jnp.sum(total, axis=0, keepdims=True)
    scale = lax.rsqrt(total / depth + 1e-06)
    t = t_ref[0]
    sums = gate = up = 0.0
    for k, (n_ref, w) in enumerate(((n0, w0), (n1, w1), (n2, w2), (n3, w3))):
        at = pl.ds(pl.multiple_of(jnp.bitwise_xor(t, k) * block, 64), block)
        n = (x_ref[at, :] * scale).astype(BF)
        n_ref[...] = n
        sums += dot(get_wide(w, 0, block, width), n, 0, 0)
        base = block * width // 128
        gate += dot(get_wide(w, base, units, block), n)
        up += dot(get_wide(w, base + units * (-(-block // 128)), units, block), n)
    bias = jnp.broadcast_to(bias_ref[...], (128, width)).T
    factor = 1.0 / math.sqrt(4 * height)
    for j in range(width // TILE):
        for i in range(height // TBLK):
            keep = mask_ref[i, j].astype(F32)
            r, c = slice(j * TILE, (j + 1) * TILE), slice(i * TBLK, (i + 1) * TBLK)
            part = jnp.maximum(sums[r, c] + bias[r, :], 0.0)
            codes_ref[r, c] = (part * part * keep).astype(BF)
            slope_ref[r, c] = part * (keep * (2.0 * factor))
    hidden_ref[...] = (jax.nn.gelu(gate, approximate=True) * up).astype(BF)


def decode_kernel(
    t_ref, codes_ref, before_ref, shifted_ref, hidden_ref, w0, w1, w2, w3, o_ref, both_ref
):
    t, layer = t_ref[0], t_ref[1]
    n = codes_ref.shape[0]
    units = hidden_ref.shape[0]
    block = o_ref.shape[0] * ROWS // 8
    both_ref[:n] = codes_ref[...]

    @pl.when(layer == 0)
    def _():
        both_ref[n:] = before_ref[...]

    @pl.when(layer != 0)
    def _():
        both_ref[n:] = shifted_ref[...]

    both, hidden = both_ref[...], hidden_ref[...]
    peers, rows, lanes = o_ref.shape
    each = block // rows
    for k, w in enumerate((w0, w1, w2, w3)):
        decoder = jnp.concatenate(
            [get_wide(w, 0, block, n), get_wide(w, block * n // 128, block, n)], axis=1
        )
        down = get_wide(w, 2 * block * n // 128, units, block)
        value = dot(decoder, both) - dot(down, hidden, 0, 0)
        spot = jnp.bitwise_xor(t, k) * each
        for i in range(each):
            for h in range(2):
                o_ref[spot + (h * peers // 2 + i)] = value[
                    i * rows : (i + 1) * rows, h * lanes : (h + 1) * lanes
                ].astype(BF)


def total_kernel(x_ref, o_ref):
    total = jnp.sum(x_ref[...].astype(F32), axis=0).astype(BF)
    o_ref[...] = jnp.broadcast_to(total[None], o_ref.shape)


def back_kernel(t_ref, e_ref, w0, w1, w2, w3, own_ref, prev_ref, e0, e1, e2, e3):
    t = t_ref[0]
    peers, rows, lanes = e_ref.shape
    n = own_ref.shape[0]
    block = e0.shape[0]
    each = block // rows
    total = 0.0
    for k, (err_ref, w) in enumerate(((e0, w0), (e1, w1), (e2, w2), (e3, w3))):
        spot = jnp.bitwise_xor(t, k) * each
        half = [
            jnp.concatenate(
                [e_ref[spot + (h * peers // 2 + i)].astype(F32) for i in range(each)], axis=0
            ).astype(BF)
            for h in range(2)
        ]
        err = jnp.concatenate(half, axis=1)
        err_ref[...] = err
        decoder = jnp.concatenate(
            [get_wide(w, 0, block, n), get_wide(w, block * n // 128, block, n)], axis=1
        )
        total += dot(decoder, err, 0, 0)
    own_ref[...] = total[:n]
    prev_ref[...] = total[n:].astype(BF)


def decoder_grads_kernel(e0, e1, e2, e3, c0, c1, c2, c3, own_ref, prev_ref):
    n = own_ref.shape[1]
    factor = 1.0 / math.sqrt(4 * e0.shape[1])
    total = 0.0
    for e, c in ((e0, c0), (e1, c1), (e2, c2), (e3, c3)):
        total += dot(e[...], c[...], 1, 1)
    own_ref[...] = total[:, :n] * factor
    prev_ref[...] = total[:, n:] * factor


def encoder_grads_kernel(n0, n1, n2, n3, p0, p1, p2, p3, grad_ref, bias_ref):
    total = bias = 0.0
    ones = jnp.ones((8, p0.shape[1]), BF)
    for n, p in ((n0, p0), (n1, p1), (n2, p2), (n3, p3)):
        total += dot(n[...], p[...], 1, 1)
        bias += dot(ones, p[...], 1, 1)
    grad_ref[...] = total
    bias_ref[...] = bias[:1]


def local(
    resid,
    norm_gain,
    prev_codes,
    feature_mask,
    w_gate,
    w_up,
    w_down,
    enc_weight,
    enc_bias,
    dec_own,
    dec_prev,
):
    height, strip = resid.shape[1:]
    peers = lax.axis_size("feat")
    width = enc_weight.shape[2]
    units = w_gate.shape[2]
    block = strip * peers // 4
    spans = -(-block // 128)
    t = 2 * lax.axis_index("tok_0") + lax.axis_index("tok_1")
    place = jnp.stack([t, lax.axis_index("layer")]).astype(jnp.int32)
    flip = lambda a: jnp.swapaxes(a[0], 0, 1)

    (copies,) = call(
        spread_kernel,
        (flip(resid), norm_gain),
        [((peers, 2 * PITCH, height // 2), BF)],
        leaving=(0,),
        plain=True,
    )
    gathered = exchange(copies)
    (second,) = call(
        pack_kernel,
        (flip(dec_own), flip(dec_prev), w_down[0]),
        [((2 * block * width // 128 + units * spans, 128), BF)],
        plain=True,
    )
    near, far = toward(second, 1), toward(second, 2)
    first, before = call(
        pack_turn_kernel,
        (enc_weight[0], flip(w_gate), flip(w_up), prev_codes),
        [((block * width // 128 + 2 * units * spans, 128), BF), ((width, height), BF)],
        plain=True,
    )
    first = gather4(first)
    *normed, codes, slope, hidden = call(
        encode_kernel,
        (place, feature_mask[0], gathered, *first, enc_bias),
        [((block, height), BF)] * 4
        + [((width, height), BF), ((width, height), F32), ((units, height), BF)],
        scratch=[pltpu.VMEM((4 * block, height), F32)],
    )
    shifted = lax.ppermute(codes, "layer", [(0, 1)])
    (far,) = call(pin_kernel, (), [], after=(slope,), through=(far,))
    second = [second, near, far, toward(far, 1)]
    parts, both = call(
        decode_kernel,
        (place, codes, before, shifted, hidden, *second),
        [((peers, ROWS, height // 2), BF), ((2 * width, height), BF)],
        leaving=(0,),
    )
    arrived = exchange(parts)
    normed = exchange4(normed)
    (copies,) = call(total_kernel, (arrived,), [(parts.shape, BF)], after=(corner(normed[1:]),), leaving=(0,))
    errors = exchange(copies)
    both = gather4(both)
    own_back, prev_back, *err = call(
        back_kernel,
        (place, errors, *second),
        [((width, height), F32), ((width, height), BF)] + [((block, height), BF)] * 4,
        after=(corner(both[1:]),),
    )
    later = lax.ppermute(prev_back, "layer", [(1, 0)])
    err[2] = toward(err[2], 2)
    (pregrad,) = call(
        pregrad_kernel,
        (own_back, later, slope),
        [((width, height), BF)],
        after=(err[2],),
    )
    pregrad = gather4(pregrad)
    (last,) = call(pin_kernel, (), [], after=(pregrad[2],), through=(err[3],))
    err[3] = toward(last, 3)
    (last,) = call(pin_kernel, (), [], after=(pregrad[1],), through=(err[1],))
    err[1] = toward(last, 1)
    grad_own, grad_prev = call(
        decoder_grads_kernel, (*err, *both), [((block, width), F32)] * 2, leaving=(0, 1)
    )
    grad_enc, grad_bias = call(
        encoder_grads_kernel,
        (*normed, *pregrad),
        [((block, width), F32), ((1, width), F32)],
        leaving=(0, 1),
    )
    return (grad_enc[None], grad_bias, grad_own.T[None], grad_prev.T[None])


def solution(mesh):
    split = Mesh(
        mesh.devices.reshape(mesh.shape["layer"], mesh.shape["feat"], 2, 2),
        ("layer", "feat", "tok_0", "tok_1"),
    )
    placed = (
        P("layer", TOK, "feat"),
        P("layer", "feat"),
        P(TOK, "feat"),
        P("layer", TOK, "feat"),
        P("layer", TOK, "feat"),
        P("layer", TOK, "feat"),
        P("layer", "feat", TOK),
        P("layer", TOK, "feat"),
        P("layer", "feat"),
        P("layer", "feat", TOK),
        P("layer", "feat", TOK),
    )
    return jax.shard_map(
        local,
        mesh=split,
        in_specs=placed,
        out_specs=(
            P("layer", TOK, "feat"),
            P("layer", "feat"),
            P("layer", "feat", TOK),
            P("layer", "feat", TOK),
        ),
        check_vma=False,
    )
```

```python
import math

import jax
import jax.numpy as jnp
from jax import lax
from jax.experimental import pallas as pl
from jax.experimental.pallas import tpu as pltpu
from jax.sharding import Mesh
from jax.sharding import PartitionSpec as P

TILE = 128
TBLK = 128
BF = jnp.bfloat16
F32 = jnp.float32
TOK = ("tok_0", "tok_1")
FEAT = ("y_1", "y_0", "z_1", "z_0")
NEAR = ("y_0", "z_0")
WIDE = ("y_1", "z_1")
PARAMS = pltpu.CompilerParams(vmem_limit_bytes=24 * 1024 * 1024)
VM = pl.BlockSpec(memory_space=pltpu.VMEM)
SM = pl.BlockSpec(memory_space=pltpu.SMEM)


ANY = pl.BlockSpec(memory_space=pl.ANY)
PITCH = 40
ROWS = 72


def call(kernel, ins, outs, after=(), through=(), scratch=(), leaving=(), plain=False):
    def held(a):
        small = plain or a.dtype == jnp.int32 or a.size < 2**15
        return a if small else pltpu.with_memory_space_constraint(a, pltpu.VMEM)

    n, p, skip = len(outs), len(through), len(ins) + len(after)
    specs = [SM if a.dtype == jnp.int32 else VM for a in ins]

    def body(*refs):
        rest = refs[skip + p :]
        kernel(*refs[: len(ins)], *rest[:n], *rest[n + p :])

    return pl.pallas_call(
        body,
        out_shape=[
            (pltpu.HBM if i in leaving else pltpu.VMEM)(*o) for i, o in enumerate(outs)
        ]
        + [pltpu.VMEM(a.shape, a.dtype) for a in through],
        in_specs=specs + [VM] * (skip - len(ins) + p),
        out_specs=[VM] * (n + p),
        input_output_aliases={skip + i: n + i for i in range(p)},
        scratch_shapes=list(scratch),
        compiler_params=PARAMS,
        name=kernel.__name__,
    )(*(held(a) for a in (*ins, *after, *through)))


def corner(arrays):
    return sum(lax.slice(a, (0, 0), (8, 128)).astype(F32) for a in arrays)


def dot(a, b, ca=1, cb=0):
    return lax.dot_general(a, b, (((ca,), (cb,)), ((), ())), preferred_element_type=F32)


def toward(x, k, axes=TOK):
    return lax.ppermute(x, axes, [(i, i ^ k) for i in range(4)])


def gather4(x):
    far = toward(x, 2)
    return [x, toward(x, 1), far, toward(far, 1)]


def exchange4(blocks, axes=TOK):
    return [blocks[0]] + [toward(blocks[k], k, axes) for k in (1, 2, 3)]


def exchange(blocks, axes=FEAT):
    return lax.all_to_all(blocks, axes, split_axis=0, concat_axis=0, tiled=True)


def spread_kernel(x_ref, gain_ref, o_ref):
    strip, height = x_ref.shape
    lanes = height // 2
    x = x_ref[...].astype(F32)
    gain = gain_ref[...].astype(F32)
    row = jnp.concatenate([gain, jnp.zeros((1, lanes - strip), F32)], axis=1)
    rest = jnp.zeros((PITCH - strip - 1, lanes), F32)
    parts = [x[:, :lanes], row, rest, x[:, lanes:], row, rest]
    o_ref[...] = jnp.broadcast_to(jnp.concatenate(parts, axis=0).astype(BF)[None], o_ref.shape)


def put_wide(o_ref, at, w):
    rows, cols = w.shape
    for c in range(0, cols, 128):
        wide = min(128, cols - c)
        o_ref[pl.ds(at, rows), pl.ds(0, wide)] = w[:, c : c + wide]
        at += rows
    return at


def get_wide(w_ref, at, rows, cols):
    pieces = [
        w_ref[pl.ds(at + rows * i, rows), : min(128, cols - 128 * i)] for i in range(-(-cols // 128))
    ]
    return jnp.concatenate(pieces, axis=1)


def pack_kernel(*refs):
    *ws, o_ref = refs
    at = 0
    for w in ws:
        at = put_wide(o_ref, at, w[...])


def pack_turn_kernel(*refs):
    *ws, x_ref, o_ref, turned_ref = refs
    pack_kernel(*ws, o_ref)
    turned_ref[...] = x_ref[...].astype(F32).T.astype(BF)


def pin_kernel(*refs):
    pass


def pregrad_kernel(own_ref, later_ref, slope_ref, o_ref):
    back = own_ref[...] + later_ref[...].astype(F32)
    o_ref[...] = (back * slope_ref[...]).astype(BF)


def encode_kernel(
    t_ref, mask_ref, g_ref, w0, w1, w2, w3, bias_ref,
    n0, n1, n2, n3, codes_ref, slope_ref, hidden_ref, x_ref,
):
    feats, _, lanes = g_ref.shape
    height = 2 * lanes
    block = n0.shape[0]
    strip = 4 * block // feats
    depth = feats * strip
    width = codes_ref.shape[0]
    units = hidden_ref.shape[0]
    gains = g_ref[:, strip, :].astype(F32).T
    total = jnp.zeros((8, height), F32)
    for f in range(feats):
        x = jnp.concatenate(
            [g_ref[f, pl.ds(0, strip), :], g_ref[f, pl.ds(PITCH, strip), :]], axis=1
        ).astype(F32)
        square = x * x
        for r in range(0, strip - 7, 8):
            total = total + square[r : r + 8]
        tail = square[strip // 8 * 8 :]
        total = total + jnp.concatenate([tail, jnp.zeros_like(tail)], axis=0)
        x_ref[pl.ds(f * strip, strip), :] = x * gains[:strip, f : f + 1]
    total = jnp.sum(total, axis=0, keepdims=True)
    scale = lax.rsqrt(total / depth + 1e-06)
    t = t_ref[0]
    sums = gate = up = 0.0
    for k, (n_ref, w) in enumerate(((n0, w0), (n1, w1), (n2, w2), (n3, w3))):
        at = pl.ds(pl.multiple_of(jnp.bitwise_xor(t, k) * block, 64), block)
        n = (x_ref[at, :] * scale).astype(BF)
        n_ref[...] = n
        sums += dot(get_wide(w, 0, block, width), n, 0, 0)
        base = block * width // 128
        gate += dot(get_wide(w, base, units, block), n)
        up += dot(get_wide(w, base + units * (-(-block // 128)), units, block), n)
    bias = jnp.broadcast_to(bias_ref[...], (128, width)).T
    factor = 1.0 / math.sqrt(4 * height)
    for j in range(width // TILE):
        for i in range(height // TBLK):
            keep = mask_ref[i, j].astype(F32)
            r, c = slice(j * TILE, (j + 1) * TILE), slice(i * TBLK, (i + 1) * TBLK)
            part = jnp.maximum(sums[r, c] + bias[r, :], 0.0)
            codes_ref[r, c] = (part * part * keep).astype(BF)
            slope_ref[r, c] = part * (keep * (2.0 * factor))
    hidden_ref[...] = (jax.nn.gelu(gate, approximate=True) * up).astype(BF)


def decode_kernel(
    t_ref, codes_ref, before_ref, shifted_ref, hidden_ref, w0, w1, w2, w3, o_ref, both_ref
):
    t, layer = t_ref[0], t_ref[1]
    n = codes_ref.shape[0]
    units = hidden_ref.shape[0]
    block = o_ref.shape[0] * ROWS // 8
    both_ref[:n] = codes_ref[...]

    @pl.when(layer == 0)
    def _():
        both_ref[n:] = before_ref[...]

    @pl.when(layer != 0)
    def _():
        both_ref[n:] = shifted_ref[...]

    both, hidden = both_ref[...], hidden_ref[...]
    peers, rows, lanes = o_ref.shape
    each = block // rows
    for k, w in enumerate((w0, w1, w2, w3)):
        decoder = jnp.concatenate(
            [get_wide(w, 0, block, n), get_wide(w, block * n // 128, block, n)], axis=1
        )
        down = get_wide(w, 2 * block * n // 128, units, block)
        value = dot(decoder, both) - dot(down, hidden, 0, 0)
        spot = jnp.bitwise_xor(t, k) * (2 * each)
        for i in range(each):
            for h in range(2):
                o_ref[spot + (h * each + i)] = value[
                    i * rows : (i + 1) * rows, h * lanes : (h + 1) * lanes
                ].astype(BF)


def total_kernel(x_ref, o_ref):
    total = jnp.sum(x_ref[...].astype(F32), axis=0).astype(BF)
    o_ref[...] = jnp.broadcast_to(total[None], o_ref.shape)


def back_kernel(
    t_ref, x0, x1, x2, x3, w0, w1, w2, w3, own_ref, prev_ref, e0, e1, e2, e3, s_ref
):
    t, near = t_ref[0], t_ref[2]
    for m, x in enumerate((x0, x1, x2, x3)):
        s_ref[jnp.bitwise_xor(near, m)] = x[...]
    n = own_ref.shape[0]
    block = e0.shape[0]
    total = 0.0
    for k, (err_ref, w) in enumerate(((e0, w0), (e1, w1), (e2, w2), (e3, w3))):
        spot = jnp.bitwise_xor(t, k)
        err = jnp.concatenate([s_ref[spot, h] for h in range(2)], axis=1)
        err_ref[...] = err
        decoder = jnp.concatenate(
            [get_wide(w, 0, block, n), get_wide(w, block * n // 128, block, n)], axis=1
        )
        total += dot(decoder, err, 0, 0)
    own_ref[...] = total[:n]
    prev_ref[...] = total[n:].astype(BF)


def decoder_grads_kernel(e0, e1, e2, e3, c0, c1, c2, c3, own_ref, prev_ref):
    n = own_ref.shape[1]
    factor = 1.0 / math.sqrt(4 * e0.shape[1])
    total = 0.0
    for e, c in ((e0, c0), (e1, c1), (e2, c2), (e3, c3)):
        total += dot(e[...], c[...], 1, 1)
    own_ref[...] = total[:, :n] * factor
    prev_ref[...] = total[:, n:] * factor


def encoder_grads_kernel(n0, n1, n2, n3, p0, p1, p2, p3, grad_ref, bias_ref):
    total = bias = 0.0
    ones = jnp.ones((8, p0.shape[1]), BF)
    for n, p in ((n0, p0), (n1, p1), (n2, p2), (n3, p3)):
        total += dot(n[...], p[...], 1, 1)
        bias += dot(ones, p[...], 1, 1)
    grad_ref[...] = total
    bias_ref[...] = bias[:1]


def local(
    resid,
    norm_gain,
    prev_codes,
    feature_mask,
    w_gate,
    w_up,
    w_down,
    enc_weight,
    enc_bias,
    dec_own,
    dec_prev,
):
    height, strip = resid.shape[1:]
    peers = lax.axis_size(FEAT)
    width = enc_weight.shape[2]
    units = w_gate.shape[2]
    block = strip * peers // 4
    spans = -(-block // 128)
    t = 2 * lax.axis_index("tok_0") + lax.axis_index("tok_1")
    near = 2 * lax.axis_index("y_0") + lax.axis_index("z_0")
    place = jnp.stack([t, lax.axis_index("layer"), near]).astype(jnp.int32)
    flip = lambda a: jnp.swapaxes(a[0], 0, 1)

    (copies,) = call(
        spread_kernel,
        (flip(resid), norm_gain),
        [((peers, 2 * PITCH, height // 2), BF)],
        leaving=(0,),
        plain=True,
    )
    gathered = exchange(copies)
    (second,) = call(
        pack_kernel,
        (flip(dec_own), flip(dec_prev), w_down[0]),
        [((2 * block * width // 128 + units * spans, 128), BF)],
        plain=True,
    )
    beside, far = toward(second, 1), toward(second, 2)
    first, before = call(
        pack_turn_kernel,
        (enc_weight[0], flip(w_gate), flip(w_up), prev_codes),
        [((block * width // 128 + 2 * units * spans, 128), BF), ((width, height), BF)],
        plain=True,
    )
    first = gather4(first)
    *normed, codes, slope, hidden = call(
        encode_kernel,
        (place, feature_mask[0], gathered, *first, enc_bias),
        [((block, height), BF)] * 4
        + [((width, height), BF), ((width, height), F32), ((units, height), BF)],
        scratch=[pltpu.VMEM((4 * block, height), F32)],
    )
    shifted = lax.ppermute(codes, "layer", [(0, 1)])
    (far,) = call(pin_kernel, (), [], after=(slope,), through=(far,))
    second = [second, beside, far, toward(far, 1)]
    parts, both = call(
        decode_kernel,
        (place, codes, before, shifted, hidden, *second),
        [((peers, ROWS, height // 2), BF), ((2 * width, height), BF)],
        leaving=(0,),
    )
    arrived = exchange(parts, NEAR + WIDE)
    normed = exchange4(normed)
    both = gather4(both)
    (copies,) = call(
        total_kernel,
        (arrived,),
        [((peers // 4, ROWS, height // 2), BF)],
        after=(corner(normed[1:] + both[1:]),),
        leaving=(0,),
    )
    slab = (2, block, height // 2)
    errors = exchange4([exchange(copies, WIDE).reshape(slab)] * 4, NEAR)
    own_back, prev_back, *err = call(
        back_kernel,
        (place, *errors, *second),
        [((width, height), F32), ((width, height), BF)] + [((block, height), BF)] * 4,
        scratch=[pltpu.VMEM((4, *slab), BF)],
    )
    later = lax.ppermute(prev_back, "layer", [(1, 0)])
    (pregrad,) = call(
        pregrad_kernel, (own_back, later, slope), [((width, height), BF)]
    )
    pregrad = gather4(pregrad)
    err[1], err[3] = call(
        pin_kernel, (), [], after=(pregrad[2],), through=(err[1], err[3])
    )
    err = exchange4(err)
    grad_own, grad_prev = call(
        decoder_grads_kernel, (*err, *both), [((block, width), F32)] * 2, leaving=(0, 1)
    )
    grad_enc, grad_bias = call(
        encoder_grads_kernel,
        (*normed, *pregrad),
        [((block, width), F32), ((1, width), F32)],
        leaving=(0, 1),
    )
    return (grad_enc[None], grad_bias, grad_own.T[None], grad_prev.T[None])


def solution(mesh):
    split = Mesh(
        mesh.devices.reshape(mesh.shape["layer"], 4, 2, 4, 2, 2, 2),
        ("layer", *FEAT, *TOK),
    )
    placed = (
        P("layer", TOK, FEAT),
        P("layer", FEAT),
        P(TOK, FEAT),
        P("layer", TOK, FEAT),
        P("layer", TOK, FEAT),
        P("layer", TOK, FEAT),
        P("layer", FEAT, TOK),
        P("layer", TOK, FEAT),
        P("layer", FEAT),
        P("layer", FEAT, TOK),
        P("layer", FEAT, TOK),
    )
    return jax.shard_map(
        local,
        mesh=split,
        in_specs=placed,
        out_specs=(
            P("layer", TOK, FEAT),
            P("layer", FEAT),
            P("layer", FEAT, TOK),
            P("layer", FEAT, TOK),
        ),
        check_vma=False,
    )
```

```python
import math

import jax
import jax.numpy as jnp
from jax import lax
from jax.experimental import pallas as pl
from jax.experimental.pallas import tpu as pltpu
from jax.sharding import Mesh
from jax.sharding import PartitionSpec as P

TILE = 128
TBLK = 128
BF = jnp.bfloat16
F32 = jnp.float32
TOK = ("tok_0", "tok_1")
PARAMS = pltpu.CompilerParams(vmem_limit_bytes=24 * 1024 * 1024)
VM = pl.BlockSpec(memory_space=pltpu.VMEM)
SM = pl.BlockSpec(memory_space=pltpu.SMEM)


ANY = pl.BlockSpec(memory_space=pl.ANY)
PITCH = 40
ROWS = 72


def call(kernel, ins, outs, after=(), through=(), scratch=(), leaving=(), plain=False):
    def held(a):
        small = plain or a.dtype == jnp.int32 or a.size < 2**15
        return a if small else pltpu.with_memory_space_constraint(a, pltpu.VMEM)

    n, p, skip = len(outs), len(through), len(ins) + len(after)
    specs = [SM if a.dtype == jnp.int32 else VM for a in ins]

    def body(*refs):
        rest = refs[skip + p :]
        kernel(*refs[: len(ins)], *rest[:n], *rest[n + p :])

    return pl.pallas_call(
        body,
        out_shape=[
            (pltpu.HBM if i in leaving else pltpu.VMEM)(*o) for i, o in enumerate(outs)
        ]
        + [pltpu.VMEM(a.shape, a.dtype) for a in through],
        in_specs=specs + [VM] * (skip - len(ins) + p),
        out_specs=[VM] * (n + p),
        input_output_aliases={skip + i: n + i for i in range(p)},
        scratch_shapes=list(scratch),
        compiler_params=PARAMS,
        name=kernel.__name__,
    )(*(held(a) for a in (*ins, *after, *through)))


def corner(arrays):
    return sum(lax.slice(a, (0, 0), (8, 128)).astype(F32) for a in arrays)


def dot(a, b, ca=1, cb=0):
    return lax.dot_general(a, b, (((ca,), (cb,)), ((), ())), preferred_element_type=F32)


def toward(x, k):
    return lax.ppermute(x, TOK, [(i, i ^ k) for i in range(4)])


def gather4(x):
    far = toward(x, 2)
    return [x, toward(x, 1), far, toward(far, 1)]


def exchange4(blocks):
    return [blocks[0]] + [toward(blocks[k], k) for k in (1, 2, 3)]


def exchange(blocks):
    return lax.all_to_all(blocks, "feat", split_axis=0, concat_axis=0, tiled=True)


def spread_kernel(x_ref, gain_ref, o_ref):
    strip, height = x_ref.shape
    lanes = height // 2
    x = x_ref[...].astype(F32)
    gain = gain_ref[...].astype(F32)
    row = jnp.concatenate([gain, jnp.zeros((1, lanes - strip), F32)], axis=1)
    rest = jnp.zeros((PITCH - strip - 1, lanes), F32)
    parts = [x[:, :lanes], row, rest, x[:, lanes:], row, rest]
    o_ref[...] = jnp.broadcast_to(jnp.concatenate(parts, axis=0).astype(BF)[None], o_ref.shape)


def put_wide(o_ref, at, w):
    rows, cols = w.shape
    for c in range(0, cols, 128):
        wide = min(128, cols - c)
        o_ref[pl.ds(at, rows), pl.ds(0, wide)] = w[:, c : c + wide]
        at += rows
    return at


def get_wide(w_ref, at, rows, cols):
    pieces = [
        w_ref[pl.ds(at + rows * i, rows), : min(128, cols - 128 * i)] for i in range(-(-cols // 128))
    ]
    return jnp.concatenate(pieces, axis=1)


def pack_kernel(*refs):
    *ws, o_ref = refs
    at = 0
    for w in ws:
        at = put_wide(o_ref, at, w[...])


def pack_turn_kernel(*refs):
    *ws, x_ref, o_ref, turned_ref = refs
    pack_kernel(*ws, o_ref)
    turned_ref[...] = x_ref[...].astype(F32).T.astype(BF)


def pin_kernel(*refs):
    pass


def pregrad_kernel(own_ref, later_ref, slope_ref, o_ref):
    back = own_ref[...] + later_ref[...].astype(F32)
    o_ref[...] = (back * slope_ref[...]).astype(BF)


def encode_kernel(
    t_ref, mask_ref, g_ref, w0, w1, w2, w3, bias_ref,
    n0, n1, n2, n3, codes_ref, slope_ref, hidden_ref, x_ref,
):
    feats, _, lanes = g_ref.shape
    height = 2 * lanes
    block = n0.shape[0]
    strip = 4 * block // feats
    depth = feats * strip
    width = codes_ref.shape[0]
    units = hidden_ref.shape[0]
    gains = g_ref[:, strip, :].astype(F32).T
    total = jnp.zeros((8, height), F32)
    for f in range(feats):
        x = jnp.concatenate(
            [g_ref[f, pl.ds(0, strip), :], g_ref[f, pl.ds(PITCH, strip), :]], axis=1
        ).astype(F32)
        square = x * x
        for r in range(0, strip - 7, 8):
            total = total + square[r : r + 8]
        tail = square[strip // 8 * 8 :]
        total = total + jnp.concatenate([tail, jnp.zeros_like(tail)], axis=0)
        x_ref[pl.ds(f * strip, strip), :] = x * gains[:strip, f : f + 1]
    total = jnp.sum(total, axis=0, keepdims=True)
    scale = lax.rsqrt(total / depth + 1e-06)
    t = t_ref[0]
    sums = gate = up = 0.0
    for k, (n_ref, w) in enumerate(((n0, w0), (n1, w1), (n2, w2), (n3, w3))):
        at = pl.ds(pl.multiple_of(jnp.bitwise_xor(t, k) * block, 64), block)
        n = (x_ref[at, :] * scale).astype(BF)
        n_ref[...] = n
        sums += dot(get_wide(w, 0, block, width), n, 0, 0)
        base = block * width // 128
        gate += dot(get_wide(w, base, units, block), n)
        up += dot(get_wide(w, base + units * (-(-block // 128)), units, block), n)
    bias = jnp.broadcast_to(bias_ref[...], (128, width)).T
    factor = 1.0 / math.sqrt(4 * height)
    for j in range(width // TILE):
        for i in range(height // TBLK):
            keep = mask_ref[i, j].astype(F32)
            r, c = slice(j * TILE, (j + 1) * TILE), slice(i * TBLK, (i + 1) * TBLK)
            part = jnp.maximum(sums[r, c] + bias[r, :], 0.0)
            codes_ref[r, c] = (part * part * keep).astype(BF)
            slope_ref[r, c] = part * (keep * (2.0 * factor))
    hidden_ref[...] = (jax.nn.gelu(gate, approximate=True) * up).astype(BF)


def decode_kernel(
    t_ref, codes_ref, before_ref, shifted_ref, hidden_ref, w0, w1, w2, w3, o_ref, both_ref
):
    t, layer = t_ref[0], t_ref[1]
    n = codes_ref.shape[0]
    units = hidden_ref.shape[0]
    block = o_ref.shape[0] * ROWS // 8
    both_ref[:n] = codes_ref[...]

    @pl.when(layer == 0)
    def _():
        both_ref[n:] = before_ref[...]

    @pl.when(layer != 0)
    def _():
        both_ref[n:] = shifted_ref[...]

    both, hidden = both_ref[...], hidden_ref[...]
    peers, rows, lanes = o_ref.shape
    each = block // rows
    for k, w in enumerate((w0, w1, w2, w3)):
        decoder = jnp.concatenate(
            [get_wide(w, 0, block, n), get_wide(w, block * n // 128, block, n)], axis=1
        )
        down = get_wide(w, 2 * block * n // 128, units, block)
        value = dot(decoder, both) - dot(down, hidden, 0, 0)
        spot = jnp.bitwise_xor(t, k) * each
        for i in range(each):
            for h in range(2):
                o_ref[spot + (h * peers // 2 + i)] = value[
                    i * rows : (i + 1) * rows, h * lanes : (h + 1) * lanes
                ].astype(BF)


def total_kernel(x_ref, o_ref):
    total = jnp.sum(x_ref[...].astype(F32), axis=0).astype(BF)
    o_ref[...] = jnp.broadcast_to(total[None], o_ref.shape)


def back_kernel(t_ref, e_ref, w0, w1, w2, w3, own_ref, prev_ref, e0, e1, e2, e3):
    t = t_ref[0]
    peers, rows, lanes = e_ref.shape
    n = own_ref.shape[0]
    block = e0.shape[0]
    each = block // rows
    total = 0.0
    for k, (err_ref, w) in enumerate(((e0, w0), (e1, w1), (e2, w2), (e3, w3))):
        spot = jnp.bitwise_xor(t, k) * each
        half = [
            jnp.concatenate(
                [e_ref[spot + (h * peers // 2 + i)].astype(F32) for i in range(each)], axis=0
            ).astype(BF)
            for h in range(2)
        ]
        err = jnp.concatenate(half, axis=1)
        err_ref[...] = err
        decoder = jnp.concatenate(
            [get_wide(w, 0, block, n), get_wide(w, block * n // 128, block, n)], axis=1
        )
        total += dot(decoder, err, 0, 0)
    own_ref[...] = total[:n]
    prev_ref[...] = total[n:].astype(BF)


def decoder_grads_kernel(e0, e1, e2, e3, c0, c1, c2, c3, own_ref, prev_ref):
    n = own_ref.shape[1]
    factor = 1.0 / math.sqrt(4 * e0.shape[1])
    total = 0.0
    for e, c in ((e0, c0), (e1, c1), (e2, c2), (e3, c3)):
        total += dot(e[...], c[...], 1, 1)
    own_ref[...] = total[:, :n] * factor
    prev_ref[...] = total[:, n:] * factor


def encoder_grads_kernel(n0, n1, n2, n3, p0, p1, p2, p3, grad_ref, bias_ref):
    total = bias = 0.0
    ones = jnp.ones((8, p0.shape[1]), BF)
    for n, p in ((n0, p0), (n1, p1), (n2, p2), (n3, p3)):
        total += dot(n[...], p[...], 1, 1)
        bias += dot(ones, p[...], 1, 1)
    grad_ref[...] = total
    bias_ref[...] = bias[:1]


def local(
    resid,
    norm_gain,
    prev_codes,
    feature_mask,
    w_gate,
    w_up,
    w_down,
    enc_weight,
    enc_bias,
    dec_own,
    dec_prev,
):
    height, strip = resid.shape[1:]
    peers = lax.axis_size("feat")
    width = enc_weight.shape[2]
    units = w_gate.shape[2]
    block = strip * peers // 4
    spans = -(-block // 128)
    t = 2 * lax.axis_index("tok_0") + lax.axis_index("tok_1")
    place = jnp.stack([t, lax.axis_index("layer")]).astype(jnp.int32)
    flip = lambda a: jnp.swapaxes(a[0], 0, 1)

    (copies,) = call(
        spread_kernel,
        (flip(resid), norm_gain),
        [((peers, 2 * PITCH, height // 2), BF)],
        leaving=(0,),
        plain=True,
    )
    gathered = exchange(copies)
    (second,) = call(
        pack_kernel,
        (flip(dec_own), flip(dec_prev), w_down[0]),
        [((2 * block * width // 128 + units * spans, 128), BF)],
        plain=True,
    )
    near, far = toward(second, 1), toward(second, 2)
    first, before = call(
        pack_turn_kernel,
        (enc_weight[0], flip(w_gate), flip(w_up), prev_codes),
        [((block * width // 128 + 2 * units * spans, 128), BF), ((width, height), BF)],
        plain=True,
    )
    first = gather4(first)
    *normed, codes, slope, hidden = call(
        encode_kernel,
        (place, feature_mask[0], gathered, *first, enc_bias),
        [((block, height), BF)] * 4
        + [((width, height), BF), ((width, height), F32), ((units, height), BF)],
        scratch=[pltpu.VMEM((4 * block, height), F32)],
    )
    shifted = lax.ppermute(codes, "layer", [(0, 1)])
    (far,) = call(pin_kernel, (), [], after=(slope,), through=(far,))
    second = [second, near, far, toward(far, 1)]
    parts, both = call(
        decode_kernel,
        (place, codes, before, shifted, hidden, *second),
        [((peers, ROWS, height // 2), BF), ((2 * width, height), BF)],
        leaving=(0,),
    )
    arrived = exchange(parts)
    normed = exchange4(normed)
    (copies,) = call(total_kernel, (arrived,), [(parts.shape, BF)], after=(corner(normed[1:]),), leaving=(0,))
    errors = exchange(copies)
    both = gather4(both)
    own_back, prev_back, *err = call(
        back_kernel,
        (place, errors, *second),
        [((width, height), F32), ((width, height), BF)] + [((block, height), BF)] * 4,
        after=(corner(both[1:]),),
    )
    later = lax.ppermute(prev_back, "layer", [(1, 0)])
    pregrad, err[1], err[3] = call(
        pregrad_kernel,
        (own_back, later, slope),
        [((width, height), BF)],
        through=(err[1], err[3]),
    )
    pregrad = gather4(pregrad)
    (err[3],) = call(pin_kernel, (), [], after=(pregrad[2],), through=(err[3],))
    err = exchange4(err)
    grad_own, grad_prev = call(
        decoder_grads_kernel, (*err, *both), [((block, width), F32)] * 2, leaving=(0, 1)
    )
    grad_enc, grad_bias = call(
        encoder_grads_kernel,
        (*normed, *pregrad),
        [((block, width), F32), ((1, width), F32)],
        leaving=(0, 1),
    )
    return (grad_enc[None], grad_bias, grad_own.T[None], grad_prev.T[None])


def solution(mesh):
    split = Mesh(
        mesh.devices.reshape(mesh.shape["layer"], mesh.shape["feat"], 2, 2),
        ("layer", "feat", "tok_0", "tok_1"),
    )
    placed = (
        P("layer", TOK, "feat"),
        P("layer", "feat"),
        P(TOK, "feat"),
        P("layer", TOK, "feat"),
        P("layer", TOK, "feat"),
        P("layer", TOK, "feat"),
        P("layer", "feat", TOK),
        P("layer", TOK, "feat"),
        P("layer", "feat"),
        P("layer", "feat", TOK),
        P("layer", "feat", TOK),
    )
    return jax.shard_map(
        local,
        mesh=split,
        in_specs=placed,
        out_specs=(
            P("layer", TOK, "feat"),
            P("layer", "feat"),
            P("layer", "feat", TOK),
            P("layer", "feat", TOK),
        ),
        check_vma=False,
    )
```
